256 devices in a mesh: ctx: 4 (over z_lo), resp: 32 (over x, y, core), head: 2 (over z_hi).
Axes of the slice: x: 4, y: 4, z: 8 (z_hi: 2, z_lo: 4; z = z_hi * 4 + z_lo), core: 2. Of those that a mesh axis runs over, the one named last changes fastest.
Arguments:
- queries: bfloat16 [32, 768, 32, 128], P('resp', 'ctx', 'head'), may hold values from -110 to 110
- grad_out: bfloat16 [32, 768, 32, 128], P('resp', 'ctx', 'head'), may hold values from -6 to 6
- resp_keys: bfloat16 [32, 768, 8, 128], P('resp', 'ctx', 'head'), may hold values from -6 to 6
- resp_values: bfloat16 [32, 768, 8, 128], P('resp', 'ctx', 'head'), may hold values from -6 to 6
- prompt_keys: bfloat16 [1536, 8, 128], P('ctx', 'head'), may hold values from -4 to 4
- prompt_values: bfloat16 [1536, 8, 128], P('ctx', 'head'), may hold values from -6 to 6
- resp_lengths: int32 [32], P('resp'), may hold values from 1 to 768, 18432 in all
Outputs:
- d_queries: bfloat16 [32, 768, 32, 128], P('resp', 'ctx', 'head')
- d_resp_keys: bfloat16 [32, 768, 8, 128], P('resp', 'ctx', 'head')
- d_resp_values: bfloat16 [32, 768, 8, 128], P('resp', 'ctx', 'head')
- d_prompt_keys: bfloat16 [1536, 8, 128], P(('ctx', 'resp'), 'head')
- d_prompt_values: bfloat16 [1536, 8, 128], P(('ctx', 'resp'), 'head')
The draws below stay inside these ranges and needn't reach their ends.
Inputs may be any that keep to these rules, and one draw needn't show every extreme that they name: `resp_lengths`: the longest response has exactly 768 positions.
All inputs are finite; a program needn't handle non-finite values. No bound on the sum of `resp_lengths` on one device may be relied on, other than what follows from the above.
Results may differ from the reference program's by a relative error of at most 0.02.
Values may be sent and summed in bfloat16 or wider, within the bound.
A program may use at most 192 MiB of HBM per device.

```python
import math
import jax
import jax.numpy as jnp
import numpy as np
from jax import lax

HQ = 32
KVH = 8
HD = 128
R_DEV = 192
PLEN = 1536
RLEN = 768
NRESP = 32
N_CTX = 4


def prompt_base(key):
    return jnp.clip(jax.random.normal(key, (PLEN, KVH, HD), jnp.float32), -4.0, 4.0)


def draw_prompt_keys(key, part):
    base = prompt_base(key)
    return base.astype(jnp.bfloat16)


def draw_queries(key, part):
    key = jax.random.fold_in(key, 12)
    fresh = jnp.clip(jax.random.normal(key, (NRESP, RLEN, HQ, HD), jnp.float32), -4.0, 4.0)
    return fresh.astype(jnp.bfloat16)


def levels(rng, shape, cuts, least, largest):
    def one(axis_at, shards_of):
        heights = jax.random.uniform(jax.random.fold_in(jax.random.fold_in(rng, 6), axis_at), (shards_of,), jnp.float32, least / len(cuts), largest / len(cuts))
        return jnp.repeat(jnp.exp(heights), shape[axis_at] // shards_of).reshape((-1,) + (1,) * (len(shape) - axis_at - 1))

    loudness = one(*cuts[0])
    for cut in cuts[1:]:
        loudness = loudness * one(*cut)
    return loudness


def length_profile(number_of, total, bound, skew):
    loads = [(1 << 20) // math.isqrt(grade ** skew) + 1 for grade in range(2, number_of + 1)]
    spare, given = total - bound - (number_of - 1), [1] * (number_of - 1)
    while spare > 0:
        candidates = [i for i in range(number_of - 1) if given[i] < bound]
        pool, remaining = sum([loads[i] for i in candidates]), spare
        for i in candidates:
            more = min(bound - given[i], max(1, remaining * loads[i] // pool), spare)
            given[i] = given[i] + more
            spare = spare - more
    return np.array([bound] + given)


def ragged(rng, number_of, total, reach, skew):
    if number_of == 2:
        one = jax.random.randint(rng, (), max(1, total - reach), min(reach, total - 1) + 1)
        return jnp.stack([one, total - one])
    lengths = jnp.asarray(length_profile(number_of, total, reach, skew), jnp.int32)
    couples = (number_of - 1) // 2
    donor, taker = lengths[1:1 + 2 * couples:2], lengths[2:2 + 2 * couples:2]
    margin = jnp.minimum(donor - 1, reach - taker)
    passed = jax.random.randint(jax.random.fold_in(rng, 1), (couples,), 0, 1 << 20) % (margin + 1)
    lengths = lengths.at[1:1 + 2 * couples:2].set(donor - passed).at[2:2 + 2 * couples:2].set(taker + passed)
    return lengths[jax.random.permutation(jax.random.fold_in(rng, 2), number_of)]


def noise(key, shape, deviation, reach, split=(), kind=jnp.bfloat16):
    values = jax.random.normal(key, shape, jnp.float32) * deviation
    if len(split) > 0:
        values = levels(key, shape, split, -0.22, 0.18) * values
    return jnp.clip(values, min=-reach, max=reach).astype(kind)


def setup_inputs(seed: int = 0) -> dict:
    streams_of = jax.random.split(jax.random.key(seed), 8)
    return {
        "queries": draw_queries(jax.random.fold_in(streams_of[7], 71), 0),
        "grad_out": noise(streams_of[1], (NRESP, RLEN, HQ, HD), 1.0, 6.0, ((0, 32), (1, 4), (2, 2))),
        "resp_keys": noise(streams_of[2], (NRESP, RLEN, KVH, HD), 1.0, 6.0, ((0, 32), (1, 4), (2, 2))),
        "resp_values": noise(streams_of[3], (NRESP, RLEN, KVH, HD), 1.0, 6.0, ((0, 32), (1, 4), (2, 2))),
        "prompt_keys": draw_prompt_keys(jax.random.fold_in(streams_of[7], 71), 0),
        "prompt_values": noise(streams_of[5], (PLEN, KVH, HD), 1.0, 6.0, ((0, 4), (1, 2))),
        "resp_lengths": ragged(streams_of[6], NRESP, NRESP * RLEN * 3 // 4, RLEN, 2).astype(jnp.int32),
    }


def allowed_keys(row_count, key_count, first_row, prompt_count, length):
    position = first_row + jnp.arange(row_count, dtype=jnp.int32)[:, None]
    key_index = jnp.arange(key_count, dtype=jnp.int32)[None, :]
    resp_index = key_index - prompt_count
    return (key_index < prompt_count) | ((resp_index <= position) & (resp_index < length))


def group_backward(query_group, grad_group, key_group, value_group, first_row, length, prompt_count):
    scale = query_group.shape[-1] ** -0.5
    scores = jnp.einsum("tqd,jd->qtj", query_group.astype(jnp.float32), key_group.astype(jnp.float32)) * scale
    allowed = allowed_keys(query_group.shape[0], key_group.shape[0], first_row, prompt_count, length)
    scores = jnp.where(allowed[None], scores, -jnp.inf)
    row_max = jnp.max(scores, axis=-1, keepdims=True)
    exponent = jnp.exp(scores - row_max)
    weights = exponent / jnp.sum(exponent, axis=-1, keepdims=True)
    weights_low = weights.astype(jnp.bfloat16)
    grad_weights = jnp.einsum("tqd,jd->qtj", grad_group.astype(jnp.float32), value_group.astype(jnp.float32))
    row_delta = jnp.sum(weights * grad_weights, axis=-1, keepdims=True)
    grad_scores = (weights * (grad_weights - row_delta) * scale).astype(jnp.bfloat16)
    grad_query = jnp.einsum("qtj,jd->tqd", grad_scores.astype(jnp.float32), key_group.astype(jnp.float32))
    grad_key = jnp.einsum("qtj,tqd->jd", grad_scores.astype(jnp.float32), query_group.astype(jnp.float32))
    grad_value = jnp.einsum("qtj,tqd->jd", weights_low.astype(jnp.float32), grad_group.astype(jnp.float32))
    return grad_query, grad_key, grad_value


def reference(queries, grad_out, resp_keys, resp_values, prompt_keys, prompt_values, resp_lengths):
    group_size = HQ // KVH

    def one_response(totals_in, inputs):
        query_rows, grad_rows, key_rows, value_rows, length = inputs
        all_keys = jnp.concatenate([prompt_keys, key_rows], 0).transpose(1, 0, 2)
        all_values = jnp.concatenate([prompt_values, value_rows], 0).transpose(1, 0, 2)
        position = jnp.arange(RLEN, dtype=jnp.int32)
        grad_rows = jnp.where((position < length)[:, None, None], grad_rows, jnp.zeros_like(grad_rows))

        def one_block(block_index):
            first_row = (block_index * R_DEV).astype(jnp.int32)
            query_block = lax.dynamic_slice_in_dim(query_rows, first_row, R_DEV, 0)
            query_block = query_block.reshape(R_DEV, KVH, group_size, HD).transpose(1, 0, 2, 3)
            grad_block = lax.dynamic_slice_in_dim(grad_rows, first_row, R_DEV, 0)
            grad_block = grad_block.reshape(R_DEV, KVH, group_size, HD).transpose(1, 0, 2, 3)

            def per_group(pieces):
                return group_backward(pieces[0], pieces[1], pieces[2], pieces[3], first_row, length, PLEN)

            grad_query, grad_key, grad_value = lax.map(per_group, (query_block, grad_block, all_keys, all_values))
            return grad_query.transpose(1, 0, 2, 3).reshape(R_DEV, HQ, HD), grad_key, grad_value

        grad_query, grad_key, grad_value = lax.map(one_block, jnp.arange(N_CTX, dtype=jnp.int32))
        grad_query = grad_query.reshape(RLEN, HQ, HD).astype(jnp.bfloat16)
        resp_key_grad = jnp.sum(grad_key[:, :, PLEN:].astype(jnp.bfloat16).astype(jnp.float32), 0)
        resp_value_grad = jnp.sum(grad_value[:, :, PLEN:].astype(jnp.bfloat16).astype(jnp.float32), 0)
        resp_key_grad = resp_key_grad.transpose(1, 0, 2).astype(jnp.bfloat16)
        resp_value_grad = resp_value_grad.transpose(1, 0, 2).astype(jnp.bfloat16)
        key_total = totals_in[0] + jnp.sum(grad_key[:, :, :PLEN], 0).transpose(1, 0, 2)
        value_total = totals_in[1] + jnp.sum(grad_value[:, :, :PLEN], 0).transpose(1, 0, 2)
        return (key_total, value_total), (grad_query, resp_key_grad, resp_value_grad)

    initial = (jnp.zeros((PLEN, KVH, HD), jnp.float32), jnp.zeros((PLEN, KVH, HD), jnp.float32))
    totals, outputs = lax.scan(one_response, initial, (queries, grad_out, resp_keys, resp_values, resp_lengths))
    return (outputs[0], outputs[1], outputs[2], totals[0].astype(jnp.bfloat16), totals[1].astype(jnp.bfloat16))
```

```python
import functools

import jax
import jax.numpy as jnp
from jax import lax
from jax.experimental import pallas as pl
from jax.experimental.pallas import tpu as pltpu
from jax.sharding import PartitionSpec as P

F32 = jnp.float32
BF16 = jnp.bfloat16
MESH = pl.DeviceIdType.MESH
SCALE = 128 ** -0.5
LOG2E = 1.4426950408889634
CEXP = SCALE * LOG2E
NG = 4
NC = 4
ROWS = 192
PROWS = 384
QROWS = 768
BLK = 384
NPB = 4
NRB = 2
PIECE = 96
LOW = -1e30


def matmul(a, b):
    return lax.dot_general(a, b, (((1,), (0,)), ((), ())), preferred_element_type=F32)


def matmul_t(a, b):
    return lax.dot_general(a, b, (((0,), (0,)), ((), ())), preferred_element_type=F32)


def kernel(
    q_hbm, do_hbm, rk_hbm, rv_hbm, pk_hbm, pv_hbm, len_ref,
    dq_out, drk_out, drv_out, dpk_out, dpv_out,
    q_raw, do_raw, rk_raw, rv_raw, pk_raw, pv_raw,
    tmp, pkv, rkv, qs, dos, e_s, w_s, m_s, d_prompt, d_resp, dq_s,
    s1, r1, s2, r2, s3, r3, sp, rp, fin_r, fin_p,
    in_sem,
    z_send, z_recv, x_send, x_recv, c_send, c_recv, k_send, k_recv,
    a_send, a_recv, b_send, b_recv, o_send, o_recv, p_send, p_recv,
):
    ctx = lax.axis_index("ctx")
    resp = lax.axis_index("resp")
    core = resp % 2
    chip = resp // 2
    cx = chip // 4
    cy = chip % 4
    other = resp + 1 - 2 * core
    is_self = (cx == 0) & (cy == 0)

    def remote(src, dst, send, recv, to):
        return pltpu.make_async_remote_copy(
            src_ref=src, dst_ref=dst, send_sem=send, recv_sem=recv,
            device_id=to, device_id_type=MESH,
        )

    def ctx_at(d):
        return (ctx + d) % NC

    def plane_at(d):
        return ((chip + d) % 16) * 2 + core

    def owner(chunk, half):
        return {"ctx": (ctx + cx) % NC, "resp": (cy * 4 + chunk) * 2 + half}

    def source(sx, kind):
        return {"ctx": (ctx + NC - sx) % NC, "resp": (sx * 4 + cx) * 2 + kind}

    barrier = pltpu.get_barrier_semaphore()

    def greet(to):
        pl.semaphore_signal(barrier, inc=1, device_id=to, device_id_type=MESH)

    loads = []
    for i, (src, dst) in enumerate(
        ((pk_hbm, pk_raw), (pv_hbm, pv_raw), (rk_hbm, rk_raw), (rv_hbm, rv_raw), (q_hbm, q_raw), (do_hbm, do_raw))
    ):
        load = pltpu.make_async_copy(src, dst, in_sem.at[i])
        load.start()
        loads.append(load)

    for d in range(1, NC):
        greet({"ctx": ctx_at(d)})

    def greet_plane(d, _):
        greet({"resp": plane_at(d)})
        return 0

    lax.fori_loop(1, 16, greet_plane, 0)
    greet({"resp": other})
    for a in range(4):
        for h in range(2):
            own_to = is_self & (core == h) if a == 0 else False

            def greet_pair(a=a, h=h):
                greet(owner(a, h))
                greet(source(a, h))

            if a == 0:
                pl.when(jnp.logical_not(own_to))(greet_pair)
            else:
                greet_pair()

    for b in range(1, NC):
        @pl.when(ctx < b)
        def _(b=b):
            for kind in range(2):
                for g in range(NG):
                    rkv[kind, g, b] = jnp.zeros((ROWS, 128), BF16)

    for kind in range(2):
        loads[kind].wait()
        raw = pk_raw if kind == 0 else pv_raw
        tmp[0 : PROWS * NG, :] = raw[...].astype(F32)
        for g in range(NG):
            pkv[kind, g, 0] = tmp[pl.ds(g, PROWS, stride=NG), :].astype(BF16).reshape(4, PIECE, 128)
    for kind in range(2):
        loads[2 + kind].wait()
        raw = rk_raw if kind == 0 else rv_raw
        tmp[0 : ROWS * NG, :] = raw[...].astype(F32)
        for g in range(NG):
            rkv[kind, g, ctx] = tmp[pl.ds(g, ROWS, stride=NG), :].astype(BF16)

    @pl.when(is_self)
    def _():
        pl.semaphore_wait(barrier, 33)

    @pl.when(jnp.logical_not(is_self))
    def _():
        pl.semaphore_wait(barrier, 35)

    def z_copy(g, d):
        return remote(
            pkv.at[core, g, 0, cx], pkv.at[core, g, NC - d, cx],
            z_send.at[g, d - 1], z_recv.at[g, NC - d - 1], {"ctx": ctx_at(d)},
        )

    def z_arrival(g, d):
        return remote(
            pkv.at[core, g, 0, cx], pkv.at[core, g, d, cx],
            z_send.at[g, d - 1], z_recv.at[g, d - 1], {"ctx": ctx_at(d)},
        )

    def x_copy(g, d):
        to = ((cx + d) % 4 * 4 + cy) * 2 + core
        return remote(
            pkv.at[core, g, pl.ds(1, 3), cx], pkv.at[core, g, pl.ds(1, 3), cx],
            x_send.at[g, d - 1], x_recv.at[g, d - 1], {"resp": to},
        )

    def x_arrival(g, d):
        sx = (cx + 4 - d) % 4
        to = ((cx + d) % 4 * 4 + cy) * 2 + core
        return remote(
            pkv.at[core, g, pl.ds(1, 3), sx], pkv.at[core, g, pl.ds(1, 3), sx],
            x_send.at[g, d - 1], x_recv.at[g, d - 1], {"resp": to},
        )

    def c_copy(g):
        return remote(
            pkv.at[core, g, pl.ds(1, 3)], pkv.at[core, g, pl.ds(1, 3)],
            c_send.at[g], c_recv.at[g], {"resp": other},
        )

    def c_arrival(g):
        return remote(
            pkv.at[1 - core, g, pl.ds(1, 3)], pkv.at[1 - core, g, pl.ds(1, 3)],
            c_send.at[g], c_recv.at[g], {"resp": other},
        )

    def k_copy(g, kind, to):
        return remote(
            rkv.at[kind, g, ctx], rkv.at[kind, g, ctx],
            k_send.at[g, kind, to], k_recv.at[g, kind, ctx], {"ctx": to},
        )

    def k_arrival(g, kind, src):
        return remote(
            rkv.at[kind, g, src], rkv.at[kind, g, src],
            k_send.at[g, kind, src], k_recv.at[g, kind, src], {"ctx": src},
        )

    def a_copy(g):
        return remote(s1.at[g], r1.at[g], a_send.at[g], a_recv.at[g], {"resp": other})

    def b_copy(g, d):
        to = (chip + d) % 16
        return remote(
            s2.at[g, to], r2.at[g, chip], b_send.at[g, d], b_recv.at[g, d], {"resp": to * 2 + core},
        )

    def b_arrival(g, d):
        src = (chip + 16 - d) % 16
        return remote(
            s2.at[g, src], r2.at[g, src], b_send.at[g, d], b_recv.at[g, d], {"resp": src * 2 + core},
        )

    def o_copy(g, chunk, half):
        return remote(
            s3.at[g, pl.ds(chunk * 24 + half * 8, 16)], r3.at[g, core, cx],
            o_send.at[g, chunk, half], o_recv.at[g, core, cx], owner(chunk, half),
        )

    def o_arrival(g, sx, kind):
        return remote(
            s3.at[g, pl.ds(0, 16)], r3.at[g, kind, sx],
            o_send.at[g, sx, kind], o_recv.at[g, kind, sx], source(sx, kind),
        )

    def p_copy(g, kind, to):
        return remote(
            sp.at[kind, g, to], rp.at[kind, g, ctx],
            p_send.at[g, kind, to], p_recv.at[g, kind, ctx], {"ctx": to},
        )

    def p_arrival(g, kind, src):
        return remote(
            sp.at[kind, g, src], rp.at[kind, g, src],
            p_send.at[g, kind, src], p_recv.at[g, kind, src], {"ctx": src},
        )

    def each_above(body):
        for c in range(1, NC):
            @pl.when(ctx < c)
            def _(c=c):
                for kind in range(2):
                    body(kind, c)

    def each_below(body):
        for c in range(NC - 1):
            @pl.when(ctx > c)
            def _(c=c):
                for kind in range(2):
                    body(kind, c)

    def send_first(g, _):
        for d in range(1, NC):
            z_copy(g, d).start()
        each_above(lambda kind, c: k_copy(g, kind, c).start())
        return 0

    lax.fori_loop(0, NG, send_first, 0)

    def forward_x(g):
        for d in range(1, NC):
            z_arrival(g, d).wait_recv()
        for d in range(1, NC):
            x_copy(g, d).start()

    def forward_core(g):
        for d in range(1, NC):
            x_arrival(g, d).wait_recv()
        c_copy(g).start()

    length = len_ref[0]
    first = ctx * ROWS

    def take_heads(load, raw, dst, keep):
        load.wait()
        tmp[...] = raw[...].astype(F32)
        for h in range(16):
            rows = tmp[pl.ds(h, ROWS, stride=16), :]
            if keep is not None:
                rows = jnp.where(keep, rows, 0.0)
            dst[h // 4, (h % 4) * ROWS : (h % 4 + 1) * ROWS, :] = rows.astype(BF16)

    take_heads(loads[4], q_raw, qs, None)
    forward_x(0)
    position = first + lax.broadcasted_iota(jnp.int32, (ROWS, 128), 0)
    take_heads(loads[5], do_raw, dos, position < length)
    forward_core(0)

    def key_block(g, kind, j):
        if j < NPB:
            return pkv[kind, g, j].reshape(BLK, 128)
        b = j - NPB
        return rkv[kind, g, 2 * b : 2 * b + 2].reshape(BLK, 128)

    def plane_send(g):
        a_copy(g).wait_recv()
        total = d_prompt[core] + r1[g].astype(F32)
        s2[g] = total.astype(BF16).reshape(16, PIECE, 128)

        def send(d, _):
            b_copy(g, d).start()
            return 0

        lax.fori_loop(1, 16, send, 0)

    def owner_send(g):
        def wait(d, _):
            b_arrival(g, d).wait_recv()
            return 0

        lax.fori_loop(1, 16, wait, 0)
        r2[g, chip] = s2[g, chip]
        total = r2[g, 0].astype(F32)
        for i in range(1, 16):
            total = total + r2[g, i].astype(F32)
        s3[g] = total * jnp.where(core == 0, SCALE, 1.0)
        for chunk in range(4):
            for half in range(2):
                if chunk == 0:
                    mine = is_self & (core == half)

                    @pl.when(mine)
                    def _(half=half):
                        r3[g, core, cx] = s3[g, half * 8 : half * 8 + 16, :]

                    @pl.when(jnp.logical_not(mine))
                    def _(half=half):
                        o_copy(g, 0, half).start()
                else:
                    o_copy(g, chunk, half).start()

    def group(g, _):
        each_below(lambda kind, c: k_arrival(g, kind, c).wait_recv())
        c_arrival(g).wait_recv()
        q = qs[g]
        do = dos[g]
        qt = q.T
        dot = do.T
        high = jnp.full((1, QROWS), LOW, F32)
        norm = jnp.zeros((1, QROWS), F32)
        delta = jnp.zeros((1, QROWS), F32)
        for j in range(NPB + NRB):
            keys = slice(j * BLK, (j + 1) * BLK)
            s = matmul(key_block(g, 0, j), qt)
            w = matmul(key_block(g, 1, j), dot)
            w_s[keys, :] = w
            if j >= NPB:
                r = lax.broadcasted_iota(jnp.int32, (BLK, QROWS), 0) + (j - NPB) * BLK
                t = lax.broadcasted_iota(jnp.int32, (1, QROWS), 1) % ROWS + first
                s = jnp.where(r <= t, s, LOW)
            new = jnp.maximum(high, jnp.max(s, axis=0, keepdims=True))
            e = jnp.exp2((s - new) * CEXP)
            e_s[keys, :] = e
            m_s[j, 0:1, :] = new
            fix = jnp.exp2((high - new) * CEXP)
            norm = norm * fix + jnp.sum(e, axis=0, keepdims=True)
            delta = delta * fix + jnp.sum(e * w, axis=0, keepdims=True)
            high = new
        inverse = 1.0 / norm
        delta = delta * inverse

        @pl.when(g < NG - 1)
        def _():
            forward_x(g + 1)

        @pl.when(g >= 1)
        def _():
            plane_send(g - 1)

        dq = jnp.zeros((128, QROWS), F32)
        for j in range(NPB + NRB):
            keys = slice(j * BLK, (j + 1) * BLK)
            weight = jnp.exp2((m_s[j, 0:1, :] - high) * CEXP) * inverse
            p = e_s[keys, :] * weight
            ds = (p * (w_s[keys, :] - delta)).astype(BF16)
            dv = matmul(p.astype(BF16), do)
            dk = matmul(ds, q)
            if j < NPB:
                d_prompt[0, keys, :] = dk
                d_prompt[1, keys, :] = dv
            else:
                b = 2 * (j - NPB)
                sp[0, g, b : b + 2] = (dk * SCALE).astype(BF16).reshape(2, ROWS, 128)
                sp[1, g, b : b + 2] = dv.astype(BF16).reshape(2, ROWS, 128)
            dq = dq + matmul_t(key_block(g, 0, j), ds)
        s1[g] = d_prompt[1 - core].astype(BF16)
        a_copy(g).start()
        each_below(lambda kind, c: p_copy(g, kind, c).start())
        dq = dq.T * SCALE
        for i in range(4):
            dq_s[pl.ds(g * 4 + i, ROWS, stride=16), :] = dq[i * ROWS : (i + 1) * ROWS, :]

        @pl.when(g < NG - 1)
        def _():
            forward_core(g + 1)

        @pl.when(g >= 1)
        def _():
            owner_send(g - 1)

        return 0

    lax.fori_loop(0, NG, group, 0)
    plane_send(NG - 1)
    dq_out[...] = dq_s[...].astype(BF16)

    def resp_wait(g, _):
        each_above(lambda kind, c: p_arrival(g, kind, c).wait_recv())
        return 0

    lax.fori_loop(0, NG, resp_wait, 0)
    for c in range(1, NC):
        @pl.when(ctx >= c)
        def _(c=c):
            for kind in range(2):
                for g in range(NG):
                    rp[kind, g, c] = jnp.zeros((ROWS, 128), BF16)

    for kind in range(2):
        for g in range(NG):
            total = sp[kind, g, ctx].astype(F32)
            for c in range(1, NC):
                total = total + rp[kind, g, c].astype(F32)
            fin_r[pl.ds(g, ROWS, stride=NG), :] = total
        out = drk_out if kind == 0 else drv_out
        out[...] = fin_r[...].astype(BF16)

    owner_send(NG - 1)

    def owner_wait(g, _):
        for sx in range(4):
            for kind in range(2):
                if sx == 0:
                    @pl.when(jnp.logical_not(is_self & (core == kind)))
                    def _(kind=kind):
                        o_arrival(g, 0, kind).wait_recv()
                else:
                    o_arrival(g, sx, kind).wait_recv()
        return 0

    lax.fori_loop(0, NG, owner_wait, 0)
    for kind in range(2):
        for g in range(NG):
            total = (r3[g, kind, 0] + r3[g, kind, 1]) + (r3[g, kind, 2] + r3[g, kind, 3])
            fin_p[pl.ds(g, 12, stride=NG), :] = jnp.where(core == 0, total[0:12], total[4:16])
        out = dpk_out if kind == 0 else dpv_out
        out[...] = fin_p[...].astype(BF16)

    def sent(g, _):
        for d in range(1, NC):
            z_copy(g, d).wait_send()
            x_copy(g, d).wait_send()
        c_copy(g).wait_send()
        a_copy(g).wait_send()
        each_above(lambda kind, c: k_copy(g, kind, c).wait_send())
        each_below(lambda kind, c: p_copy(g, kind, c).wait_send())

        def sent_plane(d, _):
            b_copy(g, d).wait_send()
            return 0

        lax.fori_loop(1, 16, sent_plane, 0)
        for chunk in range(4):
            for half in range(2):
                if chunk == 0:
                    @pl.when(jnp.logical_not(is_self & (core == half)))
                    def _(half=half):
                        o_copy(g, 0, half).wait_send()
                else:
                    o_copy(g, chunk, half).wait_send()
        return 0

    lax.fori_loop(0, NG, sent, 0)


def on_device(queries, grad_out, resp_keys, resp_values, prompt_keys, prompt_values, resp_lengths):
    dma = pltpu.SemaphoreType.DMA
    vmem = pltpu.VMEM
    outs = pl.pallas_call(
        kernel,
        out_shape=[
            jax.ShapeDtypeStruct((ROWS * 16, 128), BF16),
            jax.ShapeDtypeStruct((ROWS * NG, 128), BF16),
            jax.ShapeDtypeStruct((ROWS * NG, 128), BF16),
            jax.ShapeDtypeStruct((12 * NG, 128), BF16),
            jax.ShapeDtypeStruct((12 * NG, 128), BF16),
        ],
        in_specs=[pl.BlockSpec(memory_space=pl.ANY)] * 6 + [pl.BlockSpec(memory_space=pltpu.SMEM)],
        out_specs=[pl.BlockSpec(memory_space=pltpu.VMEM)] * 5,
        scratch_shapes=[
            vmem((ROWS * 16, 128), BF16),
            vmem((ROWS * 16, 128), BF16),
            vmem((ROWS * NG, 128), BF16),
            vmem((ROWS * NG, 128), BF16),
            vmem((PROWS * NG, 128), BF16),
            vmem((PROWS * NG, 128), BF16),
            vmem((ROWS * 16, 128), F32),
            vmem((2, NG, 4, 4, PIECE, 128), BF16),
            vmem((2, NG, NC, ROWS, 128), BF16),
            vmem((NG, QROWS, 128), BF16),
            vmem((NG, QROWS, 128), BF16),
            vmem(((NPB + NRB) * BLK, QROWS), F32),
            vmem(((NPB + NRB) * BLK, QROWS), F32),
            vmem((NPB + NRB, 8, QROWS), F32),
            vmem((2, NPB * BLK, 128), F32),
            vmem((8, 128), F32),
            vmem((ROWS * 16, 128), F32),
            vmem((NG, NPB * BLK, 128), BF16),
            vmem((NG, NPB * BLK, 128), BF16),
            vmem((NG, 16, PIECE, 128), BF16),
            vmem((NG, 16, PIECE, 128), BF16),
            vmem((NG, PIECE, 128), F32),
            vmem((NG, 2, 4, 16, 128), F32),
            vmem((2, NG, NC, ROWS, 128), BF16),
            vmem((2, NG, NC, ROWS, 128), BF16),
            vmem((ROWS * NG, 128), F32),
            vmem((12 * NG, 128), F32),
            dma((6,)),
            dma((NG, 3)), dma((NG, 3)),
            dma((NG, 3)), dma((NG, 3)),
            dma((NG,)), dma((NG,)),
            dma((NG, 2, NC)), dma((NG, 2, NC)),
            dma((NG,)), dma((NG,)),
            dma((NG, 16)), dma((NG, 16)),
            dma((NG, 4, 2)), dma((NG, 2, 4)),
            dma((NG, 2, NC)), dma((NG, 2, NC)),
        ],
        compiler_params=pltpu.CompilerParams(
            collective_id=0, has_side_effects=True, vmem_limit_bytes=56 * 1024 * 1024,
        ),
        name="attention_backward",
    )(
        queries.reshape(ROWS * 16, 128),
        grad_out.reshape(ROWS * 16, 128),
        resp_keys.reshape(ROWS * NG, 128),
        resp_values.reshape(ROWS * NG, 128),
        prompt_keys.reshape(PROWS * NG, 128),
        prompt_values.reshape(PROWS * NG, 128),
        resp_lengths,
    )
    return (
        outs[0].reshape(queries.shape),
        outs[1].reshape(resp_keys.shape),
        outs[2].reshape(resp_values.shape),
        outs[3].reshape(12, NG, 128),
        outs[4].reshape(12, NG, 128),
    )


def solution(mesh):
    heads = P("resp", "ctx", "head", None)
    prompt = P("ctx", "head", None)
    owners = P(("ctx", "resp"), "head", None)
    return jax.shard_map(
        on_device,
        mesh=mesh,
        in_specs=(heads, heads, heads, heads, prompt, prompt, P("resp")),
        out_specs=(heads, heads, heads, owners, owners),
        check_vma=False,
    )
```

```python
import functools

import jax
import jax.numpy as jnp
from jax import lax
from jax.experimental import pallas as pl
from jax.experimental.pallas import tpu as pltpu
from jax.sharding import PartitionSpec as P

F32 = jnp.float32
BF16 = jnp.bfloat16
MESH = pl.DeviceIdType.MESH
SCALE = 128 ** -0.5
LOG2E = 1.4426950408889634
CEXP = SCALE * LOG2E
NG = 4
NC = 4
ROWS = 192
PROWS = 384
QROWS = 768
BLK = 384
NPB = 4
NRB = 2
PIECE = 96
LOW = -1e30
ORDER_A = (0, 4, 5, 1, 2, 3)
ORDER_C = (4, 5, 0, 1, 2, 3)


def matmul(a, b):
    return lax.dot_general(a, b, (((1,), (0,)), ((), ())), preferred_element_type=F32)


def matmul_t(a, b):
    return lax.dot_general(a, b, (((0,), (0,)), ((), ())), preferred_element_type=F32)


def kernel(
    q_hbm, do_hbm, rk_hbm, rv_hbm, pk_hbm, pv_hbm, len_ref,
    dq_out, drk_out, drv_out, dpk_out, dpv_out,
    q_raw, do_raw, rk_raw, rv_raw, pk_raw, pv_raw,
    tmp, pkv, rkv, qs, dos, e_s, w_s, m_s, dq_s,
    s1, r1, s2, r2, s4, r4, s3, r3, sp, rp, fin_r, fin_p,
    in_sem,
    z_send, z_recv, x_send, x_recv, c_send, c_recv, k_send, k_recv,
    a_send, a_recv, b_send, b_recv, y_send, y_recv, o_send, o_recv, p_send, p_recv,
):
    ctx = lax.axis_index("ctx")
    resp = lax.axis_index("resp")
    core = resp % 2
    chip = resp // 2
    cx = chip // 4
    cy = chip % 4
    other = resp + 1 - 2 * core
    u = jnp.where(core == 0, cx, cy)
    v = jnp.where(core == 0, cy, cx)
    is_self = (u == 0) & (v == cx) & (cy == 0)

    def remote(src, dst, send, recv, to):
        return pltpu.make_async_remote_copy(
            src_ref=src, dst_ref=dst, send_sem=send, recv_sem=recv,
            device_id=to, device_id_type=MESH,
        )

    def ctx_at(d):
        return (ctx + d) % NC

    def plane_at(pu, pv):
        return (pu * (4 - 3 * core) + pv * (1 + 3 * core)) * 2 + core

    def u_at(d):
        return plane_at((u + d) % 4, v)

    def v_at(d):
        return plane_at(u, (v + d) % 4)

    def owner(chunk, half):
        return {"ctx": (ctx + u) % NC, "resp": (v * 4 + chunk) * 2 + half}

    def source(su, kind):
        at = su * (4 - 3 * kind) + cx * (1 + 3 * kind)
        return {"ctx": (ctx + NC - su) % NC, "resp": at * 2 + kind}

    barrier = pltpu.get_barrier_semaphore()

    def greet(to):
        pl.semaphore_signal(barrier, inc=1, device_id=to, device_id_type=MESH)

    loads = []
    for i, (src, dst) in enumerate(
        ((pk_hbm, pk_raw), (pv_hbm, pv_raw), (rk_hbm, rk_raw), (rv_hbm, rv_raw), (q_hbm, q_raw), (do_hbm, do_raw))
    ):
        load = pltpu.make_async_copy(src, dst, in_sem.at[i])
        load.start()
        loads.append(load)

    for d in range(1, NC):
        greet({"ctx": ctx_at(d)})

    for d in range(1, 4):
        greet({"resp": u_at(d)})
        greet({"resp": v_at(d)})
    greet({"resp": other})
    for a in range(4):
        for h in range(2):
            own_to = is_self & (core == h) if a == 0 else False

            def greet_pair(a=a, h=h):
                greet(owner(a, h))
                greet(source(a, h))

            if a == 0:
                pl.when(jnp.logical_not(own_to))(greet_pair)
            else:
                greet_pair()

    for b in range(1, NC):
        @pl.when(ctx < b)
        def _(b=b):
            for kind in range(2):
                for g in range(NG):
                    rkv[kind, g, b] = jnp.zeros((ROWS, 128), BF16)

        @pl.when((ctx >= b) | ((ctx == 0) & (b == NC - 1)))
        def _(b=b):
            for kind in range(2):
                for g in range(NG):
                    rp[kind, g, b] = jnp.zeros((ROWS, 128), BF16)

    for kind in range(2):
        loads[kind].wait()
        raw = pk_raw if kind == 0 else pv_raw
        tmp[0 : PROWS * NG, :] = raw[...].astype(F32)
        for g in range(NG):
            pkv[kind, g, 0] = tmp[pl.ds(g, PROWS, stride=NG), :].astype(BF16).reshape(4, PIECE, 128)
    for kind in range(2):
        loads[2 + kind].wait()
        raw = rk_raw if kind == 0 else rv_raw
        tmp[0 : ROWS * NG, :] = raw[...].astype(F32)
        for g in range(NG):
            rkv[kind, g, ctx] = tmp[pl.ds(g, ROWS, stride=NG), :].astype(BF16)

    @pl.when(is_self)
    def _():
        pl.semaphore_wait(barrier, 24)

    @pl.when(jnp.logical_not(is_self))
    def _():
        pl.semaphore_wait(barrier, 26)

    def z_copy(g, d):
        return remote(
            pkv.at[core, g, 0, v], pkv.at[core, g, NC - d, v],
            z_send.at[g, d - 1], z_recv.at[g, NC - d - 1], {"ctx": ctx_at(d)},
        )

    def z_arrival(g, d):
        return remote(
            pkv.at[core, g, 0, v], pkv.at[core, g, d, v],
            z_send.at[g, d - 1], z_recv.at[g, d - 1], {"ctx": ctx_at(d)},
        )

    def x_copy(g, d):
        return remote(
            pkv.at[core, g, pl.ds(1, 3), v], pkv.at[core, g, pl.ds(1, 3), v],
            x_send.at[g, d - 1], x_recv.at[g, d - 1], {"resp": v_at(d)},
        )

    def x_arrival(g, d):
        sv = (v + 4 - d) % 4
        return remote(
            pkv.at[core, g, pl.ds(1, 3), sv], pkv.at[core, g, pl.ds(1, 3), sv],
            x_send.at[g, d - 1], x_recv.at[g, d - 1], {"resp": v_at(4 - d)},
        )

    def c_copy(g):
        return remote(
            pkv.at[core, g, pl.ds(1, 3)], pkv.at[core, g, pl.ds(1, 3)],
            c_send.at[g], c_recv.at[g], {"resp": other},
        )

    def c_arrival(g):
        return remote(
            pkv.at[1 - core, g, pl.ds(1, 3)], pkv.at[1 - core, g, pl.ds(1, 3)],
            c_send.at[g], c_recv.at[g], {"resp": other},
        )

    def k_copy(g, kind, to):
        return remote(
            rkv.at[kind, g, ctx], rkv.at[kind, g, ctx],
            k_send.at[g, kind, to], k_recv.at[g, kind, ctx], {"ctx": to},
        )

    def k_arrival(g, kind, src):
        return remote(
            rkv.at[kind, g, src], rkv.at[kind, g, src],
            k_send.at[g, kind, src], k_recv.at[g, kind, src], {"ctx": src},
        )

    def k_onward(g, kind):
        return remote(
            rkv.at[kind, g, 0], rkv.at[kind, g, 0],
            k_send.at[g, kind, 0], k_recv.at[g, kind, 0], {"ctx": 3},
        )

    def a_copy(g, j):
        return remote(
            s1.at[1 - core, g, j], r1.at[g, j], a_send.at[g, j], a_recv.at[g, j], {"resp": other}
        )

    def b_copy(g, d):
        return remote(
            s2.at[g, (u + d) % 4], r2.at[g, u],
            b_send.at[g, d - 1], b_recv.at[g, d - 1], {"resp": u_at(d)},
        )

    def b_arrival(g, d):
        src = (u + 4 - d) % 4
        return remote(
            s2.at[g, src], r2.at[g, src],
            b_send.at[g, d - 1], b_recv.at[g, d - 1], {"resp": u_at(4 - d)},
        )

    def y_copy(g, d):
        return remote(
            s4.at[g, (v + d) % 4], r4.at[g, v],
            y_send.at[g, d - 1], y_recv.at[g, d - 1], {"resp": v_at(d)},
        )

    def y_arrival(g, d):
        src = (v + 4 - d) % 4
        return remote(
            s4.at[g, src], r4.at[g, src],
            y_send.at[g, d - 1], y_recv.at[g, d - 1], {"resp": v_at(4 - d)},
        )

    def o_copy(g, chunk, half):
        return remote(
            s3.at[g, chunk, half], r3.at[g, core, u],
            o_send.at[g, chunk, half], o_recv.at[g, core, u], owner(chunk, half),
        )

    def o_arrival(g, su, kind):
        return remote(
            s3.at[g, su, kind], r3.at[g, kind, su],
            o_send.at[g, su, kind], o_recv.at[g, kind, su], source(su, kind),
        )

    def p_copy(g, kind, to):
        return remote(
            sp.at[kind, g, to], rp.at[kind, g, ctx],
            p_send.at[g, kind, to], p_recv.at[g, kind, ctx], {"ctx": to},
        )

    def p_arrival(g, kind, src):
        return remote(
            sp.at[kind, g, src], rp.at[kind, g, src],
            p_send.at[g, kind, src], p_recv.at[g, kind, src], {"ctx": src},
        )

    def p_inward(g, kind):
        return remote(
            sp.at[kind, g, 0], rp.at[kind, g, 0],
            p_send.at[g, kind, 0], p_recv.at[g, kind, 0], {"ctx": 2},
        )

    def each_above(body):
        for c in range(1, NC):
            @pl.when((ctx < c) & ((ctx > 0) | (c < NC - 1)))
            def _(c=c):
                for kind in range(2):
                    body(kind, c)

    def each_below(body):
        for c in range(NC - 1):
            @pl.when((ctx > c) & ((ctx < NC - 1) | (c > 0)))
            def _(c=c):
                for kind in range(2):
                    body(kind, c)

    def send_first(g, _):
        for d in range(1, NC):
            z_copy(g, d).start()
        each_above(lambda kind, c: k_copy(g, kind, c).start())
        return 0

    lax.fori_loop(0, NG, send_first, 0)

    def onward(g):
        @pl.when(ctx == 2)
        def _():
            for kind in range(2):
                k_arrival(g, kind, 0).wait_recv()
                k_onward(g, kind).start()

    def inward(g):
        @pl.when(ctx == 2)
        def _():
            for kind in range(2):
                p_inward(g, kind).wait_recv()
                total = sp[kind, g, 0].astype(F32) + rp[kind, g, 0].astype(F32)
                sp[kind, g, 0] = total.astype(BF16)
                p_copy(g, kind, 0).start()

    def forward_x(g):
        for d in range(1, NC):
            z_arrival(g, d).wait_recv()
        for d in range(1, NC):
            x_copy(g, d).start()

    def forward_core(g):
        for d in range(1, NC):
            x_arrival(g, d).wait_recv()
        c_copy(g).start()

    length = len_ref[0]
    first = ctx * ROWS

    def take_heads(load, raw, dst, keep):
        load.wait()
        tmp[...] = raw[...].astype(F32)
        for h in range(16):
            rows = tmp[pl.ds(h, ROWS, stride=16), :]
            if keep is not None:
                rows = jnp.where(keep, rows, 0.0)
            dst[h // 4, (h % 4) * ROWS : (h % 4 + 1) * ROWS, :] = rows.astype(BF16)

    take_heads(loads[4], q_raw, qs, None)
    forward_x(0)
    position = first + lax.broadcasted_iota(jnp.int32, (ROWS, 128), 0)
    take_heads(loads[5], do_raw, dos, position < length)
    forward_core(0)
    onward(0)

    def key_block(g, kind, j):
        if j < NPB:
            return pkv[kind, g, j].reshape(BLK, 128)
        b = j - NPB
        return rkv[kind, g, 2 * b : 2 * b + 2].reshape(BLK, 128)

    def swap_send(g):
        for j in range(NPB):
            a_copy(g, j).wait_recv()
            total = s1[core, g, j].astype(F32) + r1[g, j].astype(F32)
            s2[g, j] = total.astype(BF16).reshape(4, PIECE, 128)
        for d in range(1, 4):
            b_copy(g, d).start()

    def plane_send(g):
        for d in range(1, 4):
            b_arrival(g, d).wait_recv()
        total = s2[g, u].astype(F32)
        for d in range(1, 4):
            total = total + r2[g, (u + d) % 4].astype(F32)
        s4[g] = total.astype(BF16)
        for d in range(1, 4):
            y_copy(g, d).start()

    def owner_send(g):
        for d in range(1, 4):
            y_arrival(g, d).wait_recv()
        total = s4[g, v].astype(F32)
        for d in range(1, 4):
            total = total + r4[g, (v + d) % 4].astype(F32)
        total = total * jnp.where(core == 0, SCALE, 1.0)
        for chunk in range(4):
            for half in range(2):
                at = chunk * 24 + half * 8
                s3[g, chunk, half] = total[at : at + 16].astype(BF16)
        for chunk in range(4):
            for half in range(2):
                if chunk == 0:
                    mine = is_self & (core == half)

                    @pl.when(mine)
                    def _(half=half):
                        r3[g, core, u] = s3[g, 0, half]

                    @pl.when(jnp.logical_not(mine))
                    def _(half=half):
                        o_copy(g, 0, half).start()
                else:
                    o_copy(g, chunk, half).start()

    def below_arrived(g):
        for c in range(NC - 1):
            here = (ctx > c) & (ctx != 2) if c == 0 else ctx > c

            @pl.when(here)
            def _(c=c):
                for kind in range(2):
                    k_arrival(g, kind, c).wait_recv()

    def send_below(g):
        @pl.when(ctx == 3)
        def _():
            for kind in range(2):
                p_inward(g, kind).start()

        for c in range(NC - 1):
            here = (ctx == 1) if c == 0 else ctx > c

            @pl.when(here)
            def _(c=c):
                for kind in range(2):
                    p_copy(g, kind, c).start()

    def group(g, _):
        q = qs[g]
        do = dos[g]
        qt = q.T
        dot = do.T
        high = jnp.full((1, QROWS), LOW, F32)
        norm = jnp.zeros((1, QROWS), F32)
        delta = jnp.zeros((1, QROWS), F32)
        for j in ORDER_A:
            if j == NPB:
                below_arrived(g)
            if j == 1:
                c_arrival(g).wait_recv()
            keys = slice(j * BLK, (j + 1) * BLK)
            s = matmul(key_block(g, 0, j), qt)
            w = matmul(key_block(g, 1, j), dot)
            w_s[keys, :] = w
            if j >= NPB:
                r = lax.broadcasted_iota(jnp.int32, (BLK, QROWS), 0) + (j - NPB) * BLK
                t = lax.broadcasted_iota(jnp.int32, (1, QROWS), 1) % ROWS + first
                s = jnp.where(r <= t, s, LOW)
            new = jnp.maximum(high, jnp.max(s, axis=0, keepdims=True))
            e = jnp.exp2((s - new) * CEXP)
            e_s[keys, :] = e
            m_s[j, 0:1, :] = new
            fix = jnp.exp2((high - new) * CEXP)
            norm = norm * fix + jnp.sum(e, axis=0, keepdims=True)
            delta = delta * fix + jnp.sum(e * w, axis=0, keepdims=True)
            high = new
        inverse = 1.0 / norm
        delta = delta * inverse

        @pl.when(g < NG - 1)
        def _():
            forward_x(g + 1)
            onward(g + 1)

        @pl.when(g >= 1)
        def _():
            swap_send(g - 1)

        @pl.when(g >= 2)
        def _():
            owner_send(g - 2)

        dq = jnp.zeros((128, QROWS), F32)
        for j in ORDER_C:
            keys = slice(j * BLK, (j + 1) * BLK)
            weight = jnp.exp2((m_s[j, 0:1, :] - high) * CEXP) * inverse
            p = e_s[keys, :] * weight
            ds = (p * (w_s[keys, :] - delta)).astype(BF16)
            dv = matmul(p.astype(BF16), do)
            dk = matmul(ds, q)
            if j < NPB:
                s1[0, g, j] = dk.astype(BF16)
                s1[1, g, j] = dv.astype(BF16)
                a_copy(g, j).start()
            else:
                b = 2 * (j - NPB)
                sp[0, g, b : b + 2] = (dk * SCALE).astype(BF16).reshape(2, ROWS, 128)
                sp[1, g, b : b + 2] = dv.astype(BF16).reshape(2, ROWS, 128)
                if j == NPB + NRB - 1:
                    send_below(g)
            dq = dq + matmul_t(key_block(g, 0, j), ds)
        dq = dq.T * SCALE
        for i in range(4):
            dq_s[pl.ds(g * 4 + i, ROWS, stride=16), :] = dq[i * ROWS : (i + 1) * ROWS, :]

        @pl.when(g < NG - 1)
        def _():
            forward_core(g + 1)

        @pl.when(g >= 1)
        def _():
            inward(g - 1)
            plane_send(g - 1)

        return 0

    lax.fori_loop(0, NG, group, 0)
    q_raw[...] = dq_s[...].astype(BF16)
    store = pltpu.make_async_copy(q_raw, dq_out, in_sem.at[0])
    store.start()
    swap_send(NG - 1)
    owner_send(NG - 2)
    inward(NG - 1)

    def resp_wait(g, _):
        each_above(lambda kind, c: p_arrival(g, kind, c).wait_recv())
        return 0

    lax.fori_loop(0, NG, resp_wait, 0)
    plane_send(NG - 1)
    for kind in range(2):
        for g in range(NG):
            total = sp[kind, g, ctx].astype(F32)
            for c in range(1, NC):
                total = total + rp[kind, g, c].astype(F32)
            fin_r[pl.ds(g, ROWS, stride=NG), :] = total
        out = drk_out if kind == 0 else drv_out
        out[...] = fin_r[...].astype(BF16)

    owner_send(NG - 1)

    def owner_wait(g, _):
        for sx in range(4):
            for kind in range(2):
                if sx == 0:
                    @pl.when(jnp.logical_not(is_self & (core == kind)))
                    def _(kind=kind):
                        o_arrival(g, 0, kind).wait_recv()
                else:
                    o_arrival(g, sx, kind).wait_recv()
        return 0

    lax.fori_loop(0, NG, owner_wait, 0)
    for kind in range(2):
        for g in range(NG):
            total = r3[g, kind, 0].astype(F32)
            for su in range(1, 4):
                total = total + r3[g, kind, su].astype(F32)
            fin_p[pl.ds(g, 12, stride=NG), :] = jnp.where(core == 0, total[0:12], total[4:16])
        out = dpk_out if kind == 0 else dpv_out
        out[...] = fin_p[...].astype(BF16)

    def sent(g, _):
        for d in range(1, NC):
            z_copy(g, d).wait_send()
            x_copy(g, d).wait_send()
            b_copy(g, d).wait_send()
            y_copy(g, d).wait_send()
        c_copy(g).wait_send()
        for j in range(NPB):
            a_copy(g, j).wait_send()
        each_above(lambda kind, c: k_copy(g, kind, c).wait_send())
        each_below(lambda kind, c: p_copy(g, kind, c).wait_send())

        @pl.when(ctx == 2)
        def _():
            for kind in range(2):
                k_onward(g, kind).wait_send()

        @pl.when(ctx == 3)
        def _():
            for kind in range(2):
                p_inward(g, kind).wait_send()

        for chunk in range(4):
            for half in range(2):
                if chunk == 0:
                    @pl.when(jnp.logical_not(is_self & (core == half)))
                    def _(half=half):
                        o_copy(g, 0, half).wait_send()
                else:
                    o_copy(g, chunk, half).wait_send()
        return 0

    lax.fori_loop(0, NG, sent, 0)
    store.wait()


def hand_over(*refs):
    sems = refs[-1]
    copies = [
        pltpu.make_async_copy(refs[i], refs[5 + i], sems.at[i]) for i in range(5)
    ]
    for copy in copies:
        copy.start()
    for copy in copies:
        copy.wait()


def on_device(queries, grad_out, resp_keys, resp_values, prompt_keys, prompt_values, resp_lengths):
    dma = pltpu.SemaphoreType.DMA
    vmem = pltpu.VMEM
    outs = pl.pallas_call(
        kernel,
        out_shape=[
            jax.ShapeDtypeStruct((ROWS * 16, 128), BF16),
            jax.ShapeDtypeStruct((ROWS * NG, 128), BF16),
            jax.ShapeDtypeStruct((ROWS * NG, 128), BF16),
            jax.ShapeDtypeStruct((12 * NG, 128), BF16),
            jax.ShapeDtypeStruct((12 * NG, 128), BF16),
        ],
        in_specs=[pl.BlockSpec(memory_space=pl.ANY)] * 6 + [pl.BlockSpec(memory_space=pltpu.SMEM)],
        out_specs=[pl.BlockSpec(memory_space=pl.ANY)] + [pl.BlockSpec(memory_space=pltpu.VMEM)] * 4,
        scratch_shapes=[
            vmem((ROWS * 16, 128), BF16),
            vmem((ROWS * 16, 128), BF16),
            vmem((ROWS * NG, 128), BF16),
            vmem((ROWS * NG, 128), BF16),
            vmem((PROWS * NG, 128), BF16),
            vmem((PROWS * NG, 128), BF16),
            vmem((ROWS * 16, 128), F32),
            vmem((2, NG, 4, 4, PIECE, 128), BF16),
            vmem((2, NG, NC, ROWS, 128), BF16),
            vmem((NG, QROWS, 128), BF16),
            vmem((NG, QROWS, 128), BF16),
            vmem(((NPB + NRB) * BLK, QROWS), F32),
            vmem(((NPB + NRB) * BLK, QROWS), F32),
            vmem((NPB + NRB, 8, QROWS), F32),
            vmem((ROWS * 16, 128), F32),
            vmem((2, NG, NPB, BLK, 128), BF16),
            vmem((NG, NPB, BLK, 128), BF16),
            vmem((NG, 4, 4, PIECE, 128), BF16),
            vmem((NG, 4, 4, PIECE, 128), BF16),
            vmem((NG, 4, PIECE, 128), BF16),
            vmem((NG, 4, PIECE, 128), BF16),
            vmem((NG, 4, 2, 16, 128), BF16),
            vmem((NG, 2, 4, 16, 128), BF16),
            vmem((2, NG, NC, ROWS, 128), BF16),
            vmem((2, NG, NC, ROWS, 128), BF16),
            vmem((ROWS * NG, 128), F32),
            vmem((12 * NG, 128), F32),
            dma((6,)),
            dma((NG, 3)), dma((NG, 3)),
            dma((NG, 3)), dma((NG, 3)),
            dma((NG,)), dma((NG,)),
            dma((NG, 2, NC)), dma((NG, 2, NC)),
            dma((NG, NPB)), dma((NG, NPB)),
            dma((NG, 3)), dma((NG, 3)),
            dma((NG, 3)), dma((NG, 3)),
            dma((NG, 4, 2)), dma((NG, 2, 4)),
            dma((NG, 2, NC)), dma((NG, 2, NC)),
        ],
        compiler_params=pltpu.CompilerParams(
            collective_id=0, has_side_effects=True, vmem_limit_bytes=56 * 1024 * 1024,
        ),
        name="attention_backward",
    )(
        queries.reshape(ROWS * 16, 128),
        grad_out.reshape(ROWS * 16, 128),
        resp_keys.reshape(ROWS * NG, 128),
        resp_values.reshape(ROWS * NG, 128),
        prompt_keys.reshape(PROWS * NG, 128),
        prompt_values.reshape(PROWS * NG, 128),
        resp_lengths,
    )
    anywhere = pl.BlockSpec(memory_space=pl.ANY)
    outs = pl.pallas_call(
        hand_over,
        out_shape=[jax.ShapeDtypeStruct(x.shape, x.dtype) for x in outs],
        in_specs=[anywhere] * 5,
        out_specs=[anywhere] * 5,
        scratch_shapes=[dma((5,))],
        compiler_params=pltpu.CompilerParams(vmem_limit_bytes=56 * 1024 * 1024),
        name="hand_over",
    )(*outs)
    return (
        outs[0].reshape(queries.shape),
        outs[1].reshape(resp_keys.shape),
        outs[2].reshape(resp_values.shape),
        outs[3].reshape(12, NG, 128),
        outs[4].reshape(12, NG, 128),
    )


def solution(mesh):
    heads = P("resp", "ctx", "head", None)
    prompt = P("ctx", "head", None)
    owners = P(("ctx", "resp"), "head", None)
    return jax.shard_map(
        on_device,
        mesh=mesh,
        in_specs=(heads, heads, heads, heads, prompt, prompt, P("resp")),
        out_specs=(heads, heads, heads, owners, owners),
        check_vma=False,
    )
```

```python
import functools

import jax
import jax.numpy as jnp
from jax import lax
from jax.experimental import pallas as pl
from jax.experimental.pallas import tpu as pltpu
from jax.sharding import PartitionSpec as P

F32 = jnp.float32
BF16 = jnp.bfloat16
MESH = pl.DeviceIdType.MESH
SCALE = 128 ** -0.5
LOG2E = 1.4426950408889634
CEXP = SCALE * LOG2E
NG = 4
NC = 4
ROWS = 192
PROWS = 384
QROWS = 768
BLK = 384
NPB = 4
NRB = 2
PIECE = 96
LOW = -1e30
ORDER_A = (0, 4, 5, 1, 2, 3)
ORDER_C = (0, 1, 2, 3, 4, 5)


def matmul(a, b):
    return lax.dot_general(a, b, (((1,), (0,)), ((), ())), preferred_element_type=F32)


def matmul_t(a, b):
    return lax.dot_general(a, b, (((0,), (0,)), ((), ())), preferred_element_type=F32)


def kernel(
    q_hbm, do_hbm, rk_hbm, rv_hbm, pk_hbm, pv_hbm, len_ref,
    dq_out, drk_out, drv_out, dpk_out, dpv_out,
    q_raw, do_raw, rk_raw, rv_raw, pk_raw, pv_raw,
    tmp, pkv, rkv, qs, dos, e_s, w_s, m_s, dq_s,
    s1, r1, s2, r2, s4, r4, s3, r3, sp, rp, fin_r, fin_p, fin_b,
    in_sem,
    z_send, z_recv, w_send, w_recv, x_send, x_recv, c_send, c_recv, k_send, k_recv,
    a_send, a_recv, b_send, b_recv, y_send, y_recv, o_send, o_recv, p_send, p_recv,
):
    ctx = lax.axis_index("ctx")
    resp = lax.axis_index("resp")
    core = resp % 2
    chip = resp // 2
    cx = chip // 4
    cy = chip % 4
    other = resp + 1 - 2 * core
    u = jnp.where(core == 0, cx, cy)
    v = jnp.where(core == 0, cy, cx)
    is_self = (u == 0) & (v == cx) & (cy == 0)

    def remote(src, dst, send, recv, to):
        return pltpu.make_async_remote_copy(
            src_ref=src, dst_ref=dst, send_sem=send, recv_sem=recv,
            device_id=to, device_id_type=MESH,
        )

    def ctx_at(d):
        return (ctx + d) % NC

    def plane_at(pu, pv):
        return (pu * (4 - 3 * core) + pv * (1 + 3 * core)) * 2 + core

    def u_at(d):
        return plane_at((u + d) % 4, v)

    def v_at(d):
        return plane_at(u, (v + d) % 4)

    def owner(chunk, half):
        return {"ctx": (ctx + u) % NC, "resp": (v * 4 + chunk) * 2 + half}

    def source(su, kind):
        at = su * (4 - 3 * kind) + cx * (1 + 3 * kind)
        return {"ctx": (ctx + NC - su) % NC, "resp": at * 2 + kind}

    barrier = pltpu.get_barrier_semaphore()

    def greet(to):
        pl.semaphore_signal(barrier, inc=1, device_id=to, device_id_type=MESH)

    loads = []
    for i, (src, dst) in enumerate(
        ((pk_hbm, pk_raw), (pv_hbm, pv_raw), (rk_hbm, rk_raw), (rv_hbm, rv_raw), (q_hbm, q_raw), (do_hbm, do_raw))
    ):
        load = pltpu.make_async_copy(src, dst, in_sem.at[i])
        load.start()
        loads.append(load)

    for d in range(1, NC):
        greet({"ctx": ctx_at(d)})

    for d in range(1, 4):
        greet({"resp": u_at(d)})
        greet({"resp": v_at(d)})
    greet({"resp": other})
    for a in range(4):
        for h in range(2):
            own_to = is_self & (core == h) if a == 0 else False

            def greet_pair(a=a, h=h):
                greet(owner(a, h))
                greet(source(a, h))

            if a == 0:
                pl.when(jnp.logical_not(own_to))(greet_pair)
            else:
                greet_pair()

    for b in range(1, NC):
        @pl.when(ctx < b)
        def _(b=b):
            for g in range(NG):
                rkv[g, b] = jnp.zeros((2, ROWS, 128), BF16)

        @pl.when((ctx >= b) | ((ctx == 0) & (b == NC - 1)))
        def _(b=b):
            for g in range(NG):
                rp[g, b] = jnp.zeros((2, ROWS, 128), BF16)

    for kind in range(2):
        loads[kind].wait()
        raw = pk_raw if kind == 0 else pv_raw
        tmp[0 : PROWS * NG, :] = raw[...].astype(F32)
        for g in range(NG):
            pkv[kind, g, 0] = tmp[pl.ds(g, PROWS, stride=NG), :].astype(BF16).reshape(4, PIECE, 128)
    for kind in range(2):
        loads[2 + kind].wait()
        raw = rk_raw if kind == 0 else rv_raw
        tmp[0 : ROWS * NG, :] = raw[...].astype(F32)
        for g in range(NG):
            rkv[g, ctx, kind] = tmp[pl.ds(g, ROWS, stride=NG), :].astype(BF16)

    @pl.when(is_self)
    def _():
        pl.semaphore_wait(barrier, 24)

    @pl.when(jnp.logical_not(is_self))
    def _():
        pl.semaphore_wait(barrier, 26)

    def z_copy(g, d):
        return remote(
            pkv.at[core, g, 0, v], pkv.at[core, g, NC - d, v],
            z_send.at[g, d - 1], z_recv.at[g, NC - d - 1], {"ctx": ctx_at(d)},
        )

    def z_arrival(g, d):
        return remote(
            pkv.at[core, g, 0, v], pkv.at[core, g, d, v],
            z_send.at[g, d - 1], z_recv.at[g, d - 1], {"ctx": ctx_at(d)},
        )

    def x_copy(g, d):
        return remote(
            pkv.at[core, g, pl.ds(1, 3), v], pkv.at[core, g, pl.ds(1, 3), v],
            x_send.at[g, d - 1], x_recv.at[g, d - 1], {"resp": v_at(d)},
        )

    def x_arrival(g, d):
        sv = (v + 4 - d) % 4
        return remote(
            pkv.at[core, g, pl.ds(1, 3), sv], pkv.at[core, g, pl.ds(1, 3), sv],
            x_send.at[g, d - 1], x_recv.at[g, d - 1], {"resp": v_at(4 - d)},
        )

    def w_copy(d):
        return remote(
            pkv.at[core, u, pl.ds(1, 3), v], pkv.at[core, u, pl.ds(1, 3), v],
            w_send.at[d - 1], w_recv.at[u], {"resp": u_at(d)},
        )

    def w_arrival(g):
        return remote(
            pkv.at[core, g, pl.ds(1, 3), v], pkv.at[core, g, pl.ds(1, 3), v],
            w_send.at[0], w_recv.at[g], {"resp": plane_at(g, v)},
        )

    def c_copy(g):
        return remote(
            pkv.at[core, g, pl.ds(1, 3)], pkv.at[core, g, pl.ds(1, 3)],
            c_send.at[g], c_recv.at[g], {"resp": other},
        )

    def c_arrival(g):
        return remote(
            pkv.at[1 - core, g, pl.ds(1, 3)], pkv.at[1 - core, g, pl.ds(1, 3)],
            c_send.at[g], c_recv.at[g], {"resp": other},
        )

    def k_copy(g, to):
        return remote(
            rkv.at[g, ctx], rkv.at[g, ctx], k_send.at[g, to], k_recv.at[g, ctx], {"ctx": to}
        )

    def k_arrival(g, src):
        return remote(
            rkv.at[g, src], rkv.at[g, src], k_send.at[g, src], k_recv.at[g, src], {"ctx": src}
        )

    def k_onward(g):
        return remote(
            rkv.at[g, 0], rkv.at[g, 0], k_send.at[g, 0], k_recv.at[g, 0], {"ctx": 3}
        )

    def a_copy(g, j):
        return remote(
            s1.at[1 - core, g, j], r1.at[g, j], a_send.at[g, j], a_recv.at[g, j], {"resp": other}
        )

    def b_copy(g, to):
        return remote(
            s2.at[g, to], r2.at[g, u],
            b_send.at[g, to], b_recv.at[g, u], {"resp": plane_at(to, v)},
        )

    def b_arrival(g, src):
        return remote(
            s2.at[g, src], r2.at[g, src],
            b_send.at[g, src], b_recv.at[g, src], {"resp": plane_at(src, v)},
        )

    def y_copy(g, d):
        return remote(
            s4.at[g, (v + d) % 4], r4.at[g, v],
            y_send.at[g, d - 1], y_recv.at[g, d - 1], {"resp": v_at(d)},
        )

    def y_arrival(g, d):
        src = (v + 4 - d) % 4
        return remote(
            s4.at[g, src], r4.at[g, src],
            y_send.at[g, d - 1], y_recv.at[g, d - 1], {"resp": v_at(4 - d)},
        )

    def o_copy(g, chunk, half):
        return remote(
            s3.at[g, chunk, half], r3.at[g, core, u],
            o_send.at[g, chunk, half], o_recv.at[g, core, u], owner(chunk, half),
        )

    def o_arrival(g, su, kind):
        return remote(
            s3.at[g, su, kind], r3.at[g, kind, su],
            o_send.at[g, su, kind], o_recv.at[g, kind, su], source(su, kind),
        )

    def p_copy(g, to):
        return remote(
            sp.at[g, to], rp.at[g, ctx], p_send.at[g, to], p_recv.at[g, ctx], {"ctx": to}
        )

    def p_arrival(g, src):
        return remote(
            sp.at[g, src], rp.at[g, src], p_send.at[g, src], p_recv.at[g, src], {"ctx": src}
        )

    def p_inward(g):
        return remote(
            sp.at[g, 0], rp.at[g, 0], p_send.at[g, 0], p_recv.at[g, 0], {"ctx": 2}
        )

    def each_above(body):
        for c in range(1, NC):
            @pl.when((ctx < c) & ((ctx > 0) | (c < NC - 1)))
            def _(c=c):
                body(c)

    def each_below(body):
        for c in range(NC - 1):
            @pl.when((ctx > c) & ((ctx < NC - 1) | (c > 0)))
            def _(c=c):
                body(c)

    def send_resp(g):
        for c in (2, 3, 1):
            here = (ctx < c) & (ctx > 0) if c == 3 else ctx < c

            @pl.when(here)
            def _(c=c):
                k_copy(g, c).start()

    for d in range(1, NC):
        z_copy(0, d).start()
    send_resp(0)

    def import_rest():
        for d in range(1, NC):
            z_copy(1, d).start()

        @pl.when(u > 1)
        def _():
            for d in range(1, NC):
                z_copy(u, d).start()

    def spread_u():
        @pl.when(u > 1)
        def _():
            for d in range(1, NC):
                z_arrival(u, d).wait_recv()
            for d in range(1, NC):
                w_copy(d).start()

    def onward(g):
        @pl.when(ctx == 2)
        def _():
            k_arrival(g, 0).wait_recv()
            k_onward(g).start()

    def inward(g):
        @pl.when(ctx == 2)
        def _():
            p_inward(g).wait_recv()
            total = sp[g, 0].astype(F32) + rp[g, 0].astype(F32)
            sp[g, 0] = total.astype(BF16)
            p_copy(g, 0).start()

    def forward_x(g):
        @pl.when(g <= 1)
        def _():
            for d in range(1, NC):
                z_arrival(g, d).wait_recv()

        @pl.when((g > 1) & (u != g))
        def _():
            w_arrival(g).wait_recv()

        for d in range(1, NC):
            x_copy(g, d).start()

    def forward_core(g):
        for d in range(1, NC):
            x_arrival(g, d).wait_recv()
        c_copy(g).start()

    length = len_ref[0]
    first = ctx * ROWS

    def take_heads(load, raw, dst, keep):
        load.wait()
        tmp[...] = raw[...].astype(F32)
        for h in range(16):
            rows = tmp[pl.ds(h, ROWS, stride=16), :]
            if keep is not None:
                rows = jnp.where(keep, rows, 0.0)
            dst[h // 4, (h % 4) * ROWS : (h % 4 + 1) * ROWS, :] = rows.astype(BF16)

    take_heads(loads[4], q_raw, qs, None)
    forward_x(0)
    position = first + lax.broadcasted_iota(jnp.int32, (ROWS, 128), 0)
    take_heads(loads[5], do_raw, dos, position < length)
    onward(0)
    forward_core(0)
    import_rest()
    send_resp(1)

    def key_block(g, kind, j):
        if j < NPB:
            return pkv[kind, g, j].reshape(BLK, 128)
        b = j - NPB
        return rkv[g, 2 * b : 2 * b + 2, kind].reshape(BLK, 128)

    def swap_block(g, j):
        a_copy(g, j).wait_recv()
        total = s1[core, g, j].astype(F32) + r1[g, j].astype(F32)
        s2[g, j] = total.astype(BF16).reshape(4, PIECE, 128)

        @pl.when(u != j)
        def _():
            b_copy(g, j).start()

    def plane_send(g):
        for d in range(1, 4):
            b_arrival(g, (u + d) % 4).wait_recv()
        total = s2[g, u].astype(F32)
        for d in range(1, 4):
            total = total + r2[g, (u + d) % 4].astype(F32)
        s4[g] = total.astype(BF16)
        for d in range(1, 4):
            y_copy(g, d).start()

    def owner_send(g):
        for d in range(1, 4):
            y_arrival(g, d).wait_recv()
        total = s4[g, v].astype(F32)
        for d in range(1, 4):
            total = total + r4[g, (v + d) % 4].astype(F32)
        total = total * jnp.where(core == 0, SCALE, 1.0)
        for chunk in range(4):
            for half in range(2):
                at = chunk * 24 + half * 8
                s3[g, chunk, half] = total[at : at + 16].astype(BF16)
        for chunk in range(4):
            for half in range(2):
                if chunk == 0:
                    mine = is_self & (core == half)

                    @pl.when(mine)
                    def _(half=half):
                        r3[g, core, u] = s3[g, 0, half]

                    @pl.when(jnp.logical_not(mine))
                    def _(half=half):
                        o_copy(g, 0, half).start()
                else:
                    o_copy(g, chunk, half).start()

    def below_arrived(g):
        for c in range(NC - 1):
            here = (ctx > c) & (ctx != 2) if c == 0 else ctx > c

            @pl.when(here)
            def _(c=c):
                k_arrival(g, c).wait_recv()

    def send_below(g):
        @pl.when(ctx == 3)
        def _():
            p_inward(g).start()

        for c in range(NC - 1):
            here = (ctx == 1) if c == 0 else ctx > c

            @pl.when(here)
            def _(c=c):
                p_copy(g, c).start()

    def resp_finish(g):
        each_above(lambda c: p_arrival(g, c).wait_recv())
        for kind in range(2):
            total = sp[g, ctx, kind].astype(F32)
            for c in range(1, NC):
                total = total + rp[g, c, kind].astype(F32)
            fin_r[kind, pl.ds(g, ROWS, stride=NG), :] = total

    def middle(g):
        @pl.when(g < NG - 1)
        def _():
            forward_x(g + 1)
            onward(g + 1)

        @pl.when(g == 0)
        def _():
            spread_u()

        @pl.when(g >= 1)
        def _():
            inward(g - 1)

        @pl.when(g >= 2)
        def _():
            owner_send(g - 2)

    def ending(g):
        send_below(g)
        swap_block(g, 3)

        @pl.when(g < NG - 1)
        def _():
            forward_core(g + 1)

        @pl.when(g < NG - 2)
        def _():
            send_resp(g + 2)

        @pl.when(g >= 1)
        def _():
            plane_send(g - 1)
            resp_finish(g - 1)

    def group(g, _):
        q = qs[g]
        do = dos[g]
        qt = q.T
        dot = do.T
        high = jnp.full((1, QROWS), LOW, F32)
        norm = jnp.zeros((1, QROWS), F32)
        delta = jnp.zeros((1, QROWS), F32)
        for j in ORDER_A:
            if j == NPB:
                below_arrived(g)
            if j == 1:
                c_arrival(g).wait_recv()
            keys = slice(j * BLK, (j + 1) * BLK)
            s = matmul(key_block(g, 0, j), qt)
            w = matmul(key_block(g, 1, j), dot)
            w_s[keys, :] = w
            if j >= NPB:
                r = lax.broadcasted_iota(jnp.int32, (BLK, QROWS), 0) + (j - NPB) * BLK
                t = lax.broadcasted_iota(jnp.int32, (1, QROWS), 1) % ROWS + first
                s = jnp.where(r <= t, s, LOW)
            new = jnp.maximum(high, jnp.max(s, axis=0, keepdims=True))
            e = jnp.exp2((s - new) * CEXP)
            e_s[keys, :] = e
            m_s[j, 0:1, :] = new
            fix = jnp.exp2((high - new) * CEXP)
            norm = norm * fix + jnp.sum(e, axis=0, keepdims=True)
            delta = delta * fix + jnp.sum(e * w, axis=0, keepdims=True)
            high = new
        inverse = 1.0 / norm
        delta = delta * inverse

        middle(g)
        dq = jnp.zeros((128, QROWS), F32)
        for j in ORDER_C:
            keys = slice(j * BLK, (j + 1) * BLK)
            weight = jnp.exp2((m_s[j, 0:1, :] - high) * CEXP) * inverse
            p = e_s[keys, :] * weight
            ds = (p * (w_s[keys, :] - delta)).astype(BF16)
            dv = matmul(p.astype(BF16), do)
            dk = matmul(ds, q)
            if j < NPB:
                s1[0, g, j] = dk.astype(BF16)
                s1[1, g, j] = dv.astype(BF16)
                a_copy(g, j).start()
            else:
                b = 2 * (j - NPB)
                sp[g, b : b + 2, 0] = (dk * SCALE).astype(BF16).reshape(2, ROWS, 128)
                sp[g, b : b + 2, 1] = dv.astype(BF16).reshape(2, ROWS, 128)
                if j == NPB:
                    for i in range(3):
                        swap_block(g, i)
            dq = dq + matmul_t(key_block(g, 0, j), ds)
        dq = dq.T * SCALE
        for i in range(4):
            dq_s[pl.ds(g * 4 + i, ROWS, stride=16), :] = dq[i * ROWS : (i + 1) * ROWS, :]

        ending(g)
        return 0

    lax.fori_loop(0, NG, group, 0)
    q_raw[...] = dq_s[...].astype(BF16)
    store = pltpu.make_async_copy(q_raw, dq_out, in_sem.at[0])
    store.start()
    owner_send(NG - 2)
    inward(NG - 1)
    plane_send(NG - 1)
    owner_send(NG - 1)
    resp_finish(NG - 1)
    stores = [store]
    for kind in range(2):
        held = rk_raw if kind == 0 else rv_raw
        held[...] = fin_r[kind].astype(BF16)
        stores.append(pltpu.make_async_copy(held, drk_out if kind == 0 else drv_out, in_sem.at[1 + kind]))
        stores[-1].start()

    def owner_wait(g, _):
        for sx in range(4):
            for kind in range(2):
                if sx == 0:
                    @pl.when(jnp.logical_not(is_self & (core == kind)))
                    def _(kind=kind):
                        o_arrival(g, 0, kind).wait_recv()
                else:
                    o_arrival(g, sx, kind).wait_recv()
        return 0

    lax.fori_loop(0, NG, owner_wait, 0)
    for kind in range(2):
        for g in range(NG):
            total = r3[g, kind, 0].astype(F32)
            for su in range(1, 4):
                total = total + r3[g, kind, su].astype(F32)
            fin_p[pl.ds(g, 12, stride=NG), :] = jnp.where(core == 0, total[0:12], total[4:16])
        fin_b[kind] = fin_p[...].astype(BF16)
        stores.append(pltpu.make_async_copy(fin_b.at[kind], dpk_out if kind == 0 else dpv_out, in_sem.at[3 + kind]))
        stores[-1].start()

    def sent(g, _):
        for d in range(1, NC):
            x_copy(g, d).wait_send()
            b_copy(g, (u + d) % 4).wait_send()
            y_copy(g, d).wait_send()
        c_copy(g).wait_send()
        for j in range(NPB):
            a_copy(g, j).wait_send()
        each_above(lambda c: k_copy(g, c).wait_send())
        each_below(lambda c: p_copy(g, c).wait_send())

        @pl.when(ctx == 2)
        def _():
            k_onward(g).wait_send()

        @pl.when(ctx == 3)
        def _():
            p_inward(g).wait_send()

        for chunk in range(4):
            for half in range(2):
                if chunk == 0:
                    @pl.when(jnp.logical_not(is_self & (core == half)))
                    def _(half=half):
                        o_copy(g, 0, half).wait_send()
                else:
                    o_copy(g, chunk, half).wait_send()
        return 0

    lax.fori_loop(0, NG, sent, 0)
    for d in range(1, NC):
        z_copy(0, d).wait_send()
        z_copy(1, d).wait_send()

    @pl.when(u > 1)
    def _():
        for d in range(1, NC):
            z_copy(u, d).wait_send()
            w_copy(d).wait_send()

    for copy in stores:
        copy.wait()


def hand_over(*refs):
    sems = refs[-1]
    into = [pltpu.make_async_copy(refs[i], refs[10 + i], sems.at[0, i]) for i in range(5)]
    out = [pltpu.make_async_copy(refs[10 + i], refs[5 + i], sems.at[1, i]) for i in range(5)]
    for copy in into:
        copy.start()
    for i in range(5):
        into[i].wait()
        out[i].start()
    for copy in out:
        copy.wait()


def on_device(queries, grad_out, resp_keys, resp_values, prompt_keys, prompt_values, resp_lengths):
    dma = pltpu.SemaphoreType.DMA
    vmem = pltpu.VMEM
    outs = pl.pallas_call(
        kernel,
        out_shape=[
            jax.ShapeDtypeStruct((ROWS * 16, 128), BF16),
            jax.ShapeDtypeStruct((ROWS * NG, 128), BF16),
            jax.ShapeDtypeStruct((ROWS * NG, 128), BF16),
            jax.ShapeDtypeStruct((12 * NG, 128), BF16),
            jax.ShapeDtypeStruct((12 * NG, 128), BF16),
        ],
        in_specs=[pl.BlockSpec(memory_space=pl.ANY)] * 6 + [pl.BlockSpec(memory_space=pltpu.SMEM)],
        out_specs=[pl.BlockSpec(memory_space=pl.ANY)] * 5,
        scratch_shapes=[
            vmem((ROWS * 16, 128), BF16),
            vmem((ROWS * 16, 128), BF16),
            vmem((ROWS * NG, 128), BF16),
            vmem((ROWS * NG, 128), BF16),
            vmem((PROWS * NG, 128), BF16),
            vmem((PROWS * NG, 128), BF16),
            vmem((ROWS * 16, 128), F32),
            vmem((2, NG, 4, 4, PIECE, 128), BF16),
            vmem((NG, NC, 2, ROWS, 128), BF16),
            vmem((NG, QROWS, 128), BF16),
            vmem((NG, QROWS, 128), BF16),
            vmem(((NPB + NRB) * BLK, QROWS), F32),
            vmem(((NPB + NRB) * BLK, QROWS), F32),
            vmem((NPB + NRB, 8, QROWS), F32),
            vmem((ROWS * 16, 128), F32),
            vmem((2, NG, NPB, BLK, 128), BF16),
            vmem((NG, NPB, BLK, 128), BF16),
            vmem((NG, 4, 4, PIECE, 128), BF16),
            vmem((NG, 4, 4, PIECE, 128), BF16),
            vmem((NG, 4, PIECE, 128), BF16),
            vmem((NG, 4, PIECE, 128), BF16),
            vmem((NG, 4, 2, 16, 128), BF16),
            vmem((NG, 2, 4, 16, 128), BF16),
            vmem((NG, NC, 2, ROWS, 128), BF16),
            vmem((NG, NC, 2, ROWS, 128), BF16),
            vmem((2, ROWS * NG, 128), F32),
            vmem((12 * NG, 128), F32),
            vmem((2, 12 * NG, 128), BF16),
            dma((6,)),
            dma((NG, 3)), dma((NG, 3)),
            dma((3,)), dma((NG,)),
            dma((NG, 3)), dma((NG, 3)),
            dma((NG,)), dma((NG,)),
            dma((NG, NC)), dma((NG, NC)),
            dma((NG, NPB)), dma((NG, NPB)),
            dma((NG, 4)), dma((NG, 4)),
            dma((NG, 3)), dma((NG, 3)),
            dma((NG, 4, 2)), dma((NG, 2, 4)),
            dma((NG, NC)), dma((NG, NC)),
        ],
        compiler_params=pltpu.CompilerParams(
            collective_id=0, has_side_effects=True, vmem_limit_bytes=56 * 1024 * 1024,
        ),
        name="attention_backward",
    )(
        queries.reshape(ROWS * 16, 128),
        grad_out.reshape(ROWS * 16, 128),
        resp_keys.reshape(ROWS * NG, 128),
        resp_values.reshape(ROWS * NG, 128),
        prompt_keys.reshape(PROWS * NG, 128),
        prompt_values.reshape(PROWS * NG, 128),
        resp_lengths,
    )
    anywhere = pl.BlockSpec(memory_space=pl.ANY)
    outs = pl.pallas_call(
        hand_over,
        out_shape=[jax.ShapeDtypeStruct(x.shape, x.dtype) for x in outs],
        in_specs=[anywhere] * 5,
        out_specs=[anywhere] * 5,
        scratch_shapes=[pltpu.VMEM(x.shape, x.dtype) for x in outs] + [dma((2, 5))],
        compiler_params=pltpu.CompilerParams(vmem_limit_bytes=56 * 1024 * 1024),
        name="hand_over",
    )(*outs)
    return (
        outs[0].reshape(queries.shape),
        outs[1].reshape(resp_keys.shape),
        outs[2].reshape(resp_values.shape),
        outs[3].reshape(12, NG, 128),
        outs[4].reshape(12, NG, 128),
    )


def solution(mesh):
    heads = P("resp", "ctx", "head", None)
    prompt = P("ctx", "head", None)
    owners = P(("ctx", "resp"), "head", None)
    return jax.shard_map(
        on_device,
        mesh=mesh,
        in_specs=(heads, heads, heads, heads, prompt, prompt, P("resp")),
        out_specs=(heads, heads, heads, owners, owners),
        check_vma=False,
    )
```

```python
import functools

import jax
import jax.numpy as jnp
from jax import lax
from jax.experimental import pallas as pl
from jax.experimental.pallas import tpu as pltpu
from jax.sharding import PartitionSpec as P

F32 = jnp.float32
BF16 = jnp.bfloat16
MESH = pl.DeviceIdType.MESH
SCALE = 128 ** -0.5
LOG2E = 1.4426950408889634
CEXP = SCALE * LOG2E
NG = 4
NC = 4
ROWS = 192
PROWS = 384
QROWS = 768
BLK = 384
NPB = 4
NRB = 2
PIECE = 96
LOW = -1e30
ORDER_A = (0, 1, 2, 3, 4, 5)
ORDER_C = (4, 5, 0, 1, 2, 3)


def matmul(a, b):
    return lax.dot_general(a, b, (((1,), (0,)), ((), ())), preferred_element_type=F32)


def matmul_t(a, b):
    return lax.dot_general(a, b, (((0,), (0,)), ((), ())), preferred_element_type=F32)


def kernel(
    q_hbm, do_hbm, rk_hbm, rv_hbm, pk_hbm, pv_hbm, len_ref,
    dq_out, drk_out, drv_out, dpk_out, dpv_out,
    q_raw, do_raw, rk_raw, rv_raw, pk_raw, pv_raw,
    tmp, pkv, rkv, qs, dos, e_s, w_s, m_s, ds_s, dq_s,
    s1, r1, s2, r2, s4, r4, s3, r3, sp, rp, fin_r, fin_p, fin_b,
    in_sem,
    z_send, z_recv, w_send, w_recv, x_send, x_recv, c_send, c_recv, k_send, k_recv,
    a_send, a_recv, b_send, b_recv, y_send, y_recv, o_send, o_recv, p_send, p_recv,
):
    ctx = lax.axis_index("ctx")
    resp = lax.axis_index("resp")
    core = resp % 2
    chip = resp // 2
    cx = chip // 4
    cy = chip % 4
    other = resp + 1 - 2 * core
    u = jnp.where(core == 0, cx, cy)
    v = jnp.where(core == 0, cy, cx)
    is_self = (u == 0) & (v == cx) & (cy == 0)

    def remote(src, dst, send, recv, to):
        return pltpu.make_async_remote_copy(
            src_ref=src, dst_ref=dst, send_sem=send, recv_sem=recv,
            device_id=to, device_id_type=MESH,
        )

    def ctx_at(d):
        return (ctx + d) % NC

    def plane_at(pu, pv):
        return (pu * (4 - 3 * core) + pv * (1 + 3 * core)) * 2 + core

    def u_at(d):
        return plane_at((u + d) % 4, v)

    def v_at(d):
        return plane_at(u, (v + d) % 4)

    def owner(chunk, half):
        return {"ctx": (ctx + u) % NC, "resp": (v * 4 + chunk) * 2 + half}

    def source(su, kind):
        at = su * (4 - 3 * kind) + cx * (1 + 3 * kind)
        return {"ctx": (ctx + NC - su) % NC, "resp": at * 2 + kind}

    barrier = pltpu.get_barrier_semaphore()

    def greet(to):
        pl.semaphore_signal(barrier, inc=1, device_id=to, device_id_type=MESH)

    loads = []
    for i, (src, dst) in enumerate(
        ((pk_hbm, pk_raw), (pv_hbm, pv_raw), (rk_hbm, rk_raw), (rv_hbm, rv_raw), (q_hbm, q_raw), (do_hbm, do_raw))
    ):
        load = pltpu.make_async_copy(src, dst, in_sem.at[i])
        load.start()
        loads.append(load)

    for d in range(1, NC):
        greet({"ctx": ctx_at(d)})

    for d in range(1, 4):
        greet({"resp": u_at(d)})
        greet({"resp": v_at(d)})
    greet({"resp": other})
    for a in range(4):
        for h in range(2):
            own_to = is_self & (core == h) if a == 0 else False

            def greet_pair(a=a, h=h):
                greet(owner(a, h))
                greet(source(a, h))

            if a == 0:
                pl.when(jnp.logical_not(own_to))(greet_pair)
            else:
                greet_pair()

    for b in range(1, NC):
        @pl.when(ctx < b)
        def _(b=b):
            for g in range(NG):
                rkv[g, b] = jnp.zeros((2, ROWS, 128), BF16)

        @pl.when((ctx >= b) | ((ctx == 0) & (b == NC - 1)))
        def _(b=b):
            for g in range(NG):
                rp[g, b] = jnp.zeros((2, ROWS, 128), BF16)

    for kind in range(2):
        loads[kind].wait()
        raw = pk_raw if kind == 0 else pv_raw
        tmp[0 : PROWS * NG, :] = raw[...].astype(F32)
        for g in range(NG):
            pkv[kind, g, 0] = tmp[pl.ds(g, PROWS, stride=NG), :].astype(BF16).reshape(4, PIECE, 128)
    for kind in range(2):
        loads[2 + kind].wait()
        raw = rk_raw if kind == 0 else rv_raw
        tmp[0 : ROWS * NG, :] = raw[...].astype(F32)
        for g in range(NG):
            rkv[g, ctx, kind] = tmp[pl.ds(g, ROWS, stride=NG), :].astype(BF16)

    @pl.when(is_self)
    def _():
        pl.semaphore_wait(barrier, 24)

    @pl.when(jnp.logical_not(is_self))
    def _():
        pl.semaphore_wait(barrier, 26)

    def z_copy(g, d):
        return remote(
            pkv.at[core, g, 0, v], pkv.at[core, g, NC - d, v],
            z_send, z_recv.at[g], {"ctx": ctx_at(d)},
        )

    def arrived(ref, sem):
        remote(ref, ref, z_send, sem, {"resp": other}).wait_recv()

    def left(ref, sem):
        remote(ref, ref, sem, z_recv.at[0], {"resp": other}).wait_send()

    def x_copy(g, d):
        part = pkv.at[core, g, pl.ds(1, 3), v]
        return remote(part, part, x_send, x_recv.at[g], {"resp": v_at(d)})

    def w_copy(d):
        part = pkv.at[core, u, pl.ds(1, 3), v]
        return remote(part, part, w_send, w_recv.at[u], {"resp": u_at(d)})

    def c_copy(g):
        part = pkv.at[core, g, pl.ds(1, 3)]
        return remote(part, part, c_send, c_recv.at[g], {"resp": other})

    def k_copy(g, to):
        return remote(
            rkv.at[g, ctx], rkv.at[g, ctx],
            k_send, k_recv.at[g, jnp.minimum(ctx, 1)], {"ctx": to},
        )

    def k_onward(g):
        return remote(rkv.at[g, 0], rkv.at[g, 0], k_send, k_recv.at[g, 0], {"ctx": 3})

    def a_copy(g, j):
        return remote(
            s1.at[1 - core, g, j], r1.at[g, j], a_send, a_recv.at[g, j // 3], {"resp": other}
        )

    def b_copy(g, to):
        return remote(
            s2.at[g, to], r2.at[g, u], b_send, b_recv.at[g], {"resp": plane_at(to, v)}
        )

    def y_copy(g, d):
        return remote(s4.at[g, (v + d) % 4], r4.at[g, v], y_send, y_recv.at[g], {"resp": v_at(d)})

    def o_copy(g, chunk, half):
        return remote(
            s3.at[g * 8 + chunk * 2 + half], r3.at[g * 8 + core * 4 + u],
            o_send, o_recv, owner(chunk, half),
        )

    def p_copy(g, to):
        return remote(
            sp.at[g, to], rp.at[g, ctx], p_send, p_recv.at[g, 1], {"ctx": to}
        )

    def p_inward(g):
        return remote(sp.at[g, 0], rp.at[g, 0], p_send, p_recv.at[g, 0], {"ctx": 2})

    def send_resp(g):
        for c in (2, 3, 1):
            here = (ctx < c) & (ctx > 0) if c == 3 else ctx < c

            @pl.when(here)
            def _(c=c):
                k_copy(g, c).start()

    for d in range(1, NC):
        z_copy(0, d).start()

    @pl.when(u > 0)
    def _():
        for d in range(1, NC):
            z_copy(u, d).start()

    def spread_u():
        @pl.when(u > 0)
        def _():
            arrived(pkv.at[core, u, pl.ds(1, 3), v], z_recv.at[u])
            for d in range(1, NC):
                w_copy(d).start()

    def onward(g):
        @pl.when(ctx == 2)
        def _():
            arrived(rkv.at[g, 0], k_recv.at[g, 0])
            k_onward(g).start()

    def inward(g):
        @pl.when(ctx == 2)
        def _():
            arrived(rp.at[g, 0], p_recv.at[g, 0])
            total = sp[g, 0].astype(F32) + rp[g, 0].astype(F32)
            sp[g, 0] = total.astype(BF16)
            p_copy(g, 0).start()

    def forward_x(g):
        if g == 0:
            arrived(pkv.at[core, g, pl.ds(1, 3), v], z_recv.at[g])
        else:
            @pl.when(u != g)
            def _():
                arrived(pkv.at[core, g, pl.ds(1, 3), v], w_recv.at[g])

        for d in range(1, NC):
            x_copy(g, d).start()

    def forward_core(g):
        arrived(pkv.at[core, g, pl.ds(1, 3), pl.ds(0, 3)], x_recv.at[g])
        c_copy(g).start()

    length = len_ref[0]
    first = ctx * ROWS

    def take_heads(load, raw, dst, keep):
        load.wait()
        tmp[...] = raw[...].astype(F32)
        for h in range(16):
            rows = tmp[pl.ds(h, ROWS, stride=16), :]
            if keep is not None:
                rows = jnp.where(keep, rows, 0.0)
            dst[h // 4, (h % 4) * ROWS : (h % 4 + 1) * ROWS, :] = rows.astype(BF16)

    take_heads(loads[4], q_raw, qs, None)
    send_resp(0)
    forward_x(0)
    spread_u()
    position = first + lax.broadcasted_iota(jnp.int32, (ROWS, 128), 0)
    take_heads(loads[5], do_raw, dos, position < length)
    forward_core(0)
    onward(0)
    send_resp(1)
    forward_x(1)

    def key_block(g, kind, j):
        if j < NPB:
            return pkv[kind, g, j].reshape(BLK, 128)
        b = j - NPB
        return rkv[g, 2 * b : 2 * b + 2, kind].reshape(BLK, 128)

    def swap_blocks(g, blocks):
        first_block, last_block = blocks[0], blocks[-1]
        arrived(r1.at[g, pl.ds(first_block, len(blocks))], a_recv.at[g, last_block // 3])
        for j in blocks:
            total = s1[core, g, j].astype(F32) + r1[g, j].astype(F32)
            s2[g, j] = total.astype(BF16).reshape(4, PIECE, 128)

            @pl.when(u != j)
            def _(j=j):
                b_copy(g, j).start()

    def plane_send(g):
        arrived(r2.at[g, pl.ds(0, 3)], b_recv.at[g])
        total = s2[g, u].astype(F32)
        for d in range(1, 4):
            total = total + r2[g, (u + d) % 4].astype(F32)
        s4[g] = total.astype(BF16)
        for d in range(1, 4):
            y_copy(g, d).start()

    def owner_send(g):
        arrived(r4.at[g, pl.ds(0, 3)], y_recv.at[g])
        total = s4[g, v].astype(F32)
        for d in range(1, 4):
            total = total + r4[g, (v + d) % 4].astype(F32)
        total = total * jnp.where(core == 0, SCALE, 1.0)
        for chunk in range(4):
            for half in range(2):
                at = chunk * 24 + half * 8
                s3[g * 8 + chunk * 2 + half] = total[at : at + 16].astype(BF16)
        for chunk in range(4):
            for half in range(2):
                if chunk == 0:
                    mine = is_self & (core == half)

                    @pl.when(mine)
                    def _(half=half):
                        r3[g * 8 + core * 4 + u] = s3[g * 8 + half]

                    @pl.when(jnp.logical_not(mine))
                    def _(half=half):
                        o_copy(g, 0, half).start()
                else:
                    o_copy(g, chunk, half).start()

    def below_arrived(g):
        @pl.when((ctx == 1) | (ctx == 3))
        def _():
            arrived(rkv.at[g, 0], k_recv.at[g, 0])

        @pl.when(ctx == 2)
        def _():
            arrived(rkv.at[g, 1], k_recv.at[g, 1])

        @pl.when(ctx == 3)
        def _():
            arrived(rkv.at[g, pl.ds(1, 2)], k_recv.at[g, 1])

    def send_below(g):
        @pl.when(ctx == 3)
        def _():
            p_inward(g).start()

        for c in range(NC - 1):
            here = (ctx == 1) if c == 0 else ctx > c

            @pl.when(here)
            def _(c=c):
                p_copy(g, c).start()

    def resp_finish(g):
        @pl.when(ctx < 2)
        def _():
            arrived(rp.at[g, pl.ds(0, 2)], p_recv.at[g, 1])

        @pl.when(ctx == 2)
        def _():
            arrived(rp.at[g, 3], p_recv.at[g, 1])

        for kind in range(2):
            total = sp[g, ctx, kind].astype(F32)
            for c in range(1, NC):
                total = total + rp[g, c, kind].astype(F32)
            fin_r[kind, pl.ds(g, ROWS, stride=NG), :] = total

    def middle(g):
        @pl.when(g == 0)
        def _():
            forward_x(2)

        @pl.when(g >= 1)
        def _():
            inward(g - 1)

        @pl.when(g >= 2)
        def _():
            owner_send(g - 2)

    def later(g):
        send_below(g)

        @pl.when(g < NG - 1)
        def _():
            forward_core(g + 1)
            onward(g + 1)

        @pl.when(g < NG - 2)
        def _():
            send_resp(g + 2)

        @pl.when(g >= 1)
        def _():
            plane_send(g - 1)

    def ending(g):
        @pl.when(g == 0)
        def _():
            forward_x(3)

        swap_blocks(g, (3,))

        @pl.when(g >= 1)
        def _():
            resp_finish(g - 1)

    def group(g, _):
        q = qs[g]
        do = dos[g]
        qt = q.T
        dot = do.T
        high = jnp.full((1, QROWS), LOW, F32)
        norm = jnp.zeros((1, QROWS), F32)
        delta = jnp.zeros((1, QROWS), F32)
        for j in ORDER_A:
            if j == NPB:
                below_arrived(g)
            if j == 1:
                arrived(pkv.at[1 - core, g, pl.ds(1, 3)], c_recv.at[g])
            keys = slice(j * BLK, (j + 1) * BLK)
            s = matmul(key_block(g, 0, j), qt)
            w = matmul(key_block(g, 1, j), dot)
            w_s[keys, :] = w
            if j >= NPB:
                r = lax.broadcasted_iota(jnp.int32, (BLK, QROWS), 0) + (j - NPB) * BLK
                t = lax.broadcasted_iota(jnp.int32, (1, QROWS), 1) % ROWS + first
                s = jnp.where(r <= t, s, LOW)
            new = jnp.maximum(high, jnp.max(s, axis=0, keepdims=True))
            e = jnp.exp2((s - new) * CEXP)
            e_s[keys, :] = e
            m_s[j, 0:1, :] = new
            fix = jnp.exp2((high - new) * CEXP)
            norm = norm * fix + jnp.sum(e, axis=0, keepdims=True)
            delta = delta * fix + jnp.sum(e * w, axis=0, keepdims=True)
            high = new
        inverse = 1.0 / norm
        delta = delta * inverse

        middle(g)
        for j in ORDER_C:
            keys = slice(j * BLK, (j + 1) * BLK)
            weight = jnp.exp2((m_s[j, 0:1, :] - high) * CEXP) * inverse
            p = e_s[keys, :] * weight
            ds = (p * (w_s[keys, :] - delta)).astype(BF16)
            dv = matmul(p.astype(BF16), do)
            dk = matmul(ds, q)
            if j < NPB:
                s1[0, g, j] = dk.astype(BF16)
                s1[1, g, j] = dv.astype(BF16)
                a_copy(g, j).start()
                if j == NPB - 1:
                    swap_blocks(g, (0, 1, 2))
            else:
                b = 2 * (j - NPB)
                sp[g, b : b + 2, 0] = (dk * SCALE).astype(BF16).reshape(2, ROWS, 128)
                sp[g, b : b + 2, 1] = dv.astype(BF16).reshape(2, ROWS, 128)
                if j == NPB + NRB - 1:
                    later(g)
            ds_s[g, keys, :] = ds
        ending(g)
        return 0

    lax.fori_loop(0, NG, group, 0)
    def query_part(g):
        dq = jnp.zeros((128, QROWS), F32)
        for j in range(NPB + NRB):
            dq = dq + matmul_t(key_block(g, 0, j), ds_s[g, j * BLK : (j + 1) * BLK, :])
        dq = dq.T * SCALE
        for i in range(4):
            dq_s[pl.ds(g * 4 + i, ROWS, stride=16), :] = dq[i * ROWS : (i + 1) * ROWS, :]

    query_part(0)
    owner_send(NG - 2)
    inward(NG - 1)
    query_part(1)
    query_part(2)
    plane_send(NG - 1)
    query_part(3)
    q_raw[...] = dq_s[...].astype(BF16)
    store = pltpu.make_async_copy(q_raw, dq_out, in_sem.at[0])
    store.start()
    owner_send(NG - 1)
    resp_finish(NG - 1)
    stores = [store]
    for kind in range(2):
        held = rk_raw if kind == 0 else rv_raw
        held[...] = fin_r[kind].astype(BF16)
        stores.append(pltpu.make_async_copy(held, drk_out if kind == 0 else drv_out, in_sem.at[1 + kind]))
        stores[-1].start()

    @pl.when(u == 0)
    def _():
        left(pkv.at[core, 0, pl.ds(0, 3), 0], z_send)

    @pl.when(u > 0)
    def _():
        left(pkv.at[core, 0, pl.ds(0, 3), pl.ds(0, 2)], z_send)
        left(pkv.at[core, 0, pl.ds(1, 3), pl.ds(0, 3)], w_send)

    left(pkv.at[core, :, pl.ds(1, 3), pl.ds(0, 3)], x_send)
    left(pkv.at[core, :, pl.ds(1, 3)], c_send)

    @pl.when(ctx < 3)
    def _():
        left(rkv.at[:, pl.ds(0, 2)], k_send)

    left(s1.at[0], a_send)
    left(s2.at[:, pl.ds(0, 3)], b_send)
    left(s4.at[:, pl.ds(0, 3)], y_send)
    for c in range(1, NC):
        @pl.when(ctx == c)
        def _(c=c):
            left(sp.at[:, pl.ds(0, c)], p_send)

    @pl.when(is_self)
    def _():
        left(s3.at[pl.ds(0, 28)], o_send)
        arrived(r3.at[pl.ds(0, 28)], o_recv)

    @pl.when(jnp.logical_not(is_self))
    def _():
        left(s3, o_send)
        arrived(r3, o_recv)

    for kind in range(2):
        for g in range(NG):
            total = r3[g * 8 + kind * 4].astype(F32)
            for su in range(1, 4):
                total = total + r3[g * 8 + kind * 4 + su].astype(F32)
            fin_p[pl.ds(g, 12, stride=NG), :] = jnp.where(core == 0, total[0:12], total[4:16])
        fin_b[kind] = fin_p[...].astype(BF16)
        stores.append(pltpu.make_async_copy(fin_b.at[kind], dpk_out if kind == 0 else dpv_out, in_sem.at[3 + kind]))
        stores[-1].start()

    for copy in stores:
        copy.wait()


def hand_over(*refs):
    sems = refs[-1]
    into = [pltpu.make_async_copy(refs[i], refs[10 + i], sems.at[0, i]) for i in range(5)]
    out = [pltpu.make_async_copy(refs[10 + i], refs[5 + i], sems.at[1, i]) for i in range(5)]
    for copy in into:
        copy.start()
    for i in range(5):
        into[i].wait()
        out[i].start()
    for copy in out:
        copy.wait()


def on_device(queries, grad_out, resp_keys, resp_values, prompt_keys, prompt_values, resp_lengths):
    dma = pltpu.SemaphoreType.DMA
    vmem = pltpu.VMEM
    outs = pl.pallas_call(
        kernel,
        out_shape=[
            jax.ShapeDtypeStruct((ROWS * 16, 128), BF16),
            jax.ShapeDtypeStruct((ROWS * NG, 128), BF16),
            jax.ShapeDtypeStruct((ROWS * NG, 128), BF16),
            jax.ShapeDtypeStruct((12 * NG, 128), BF16),
            jax.ShapeDtypeStruct((12 * NG, 128), BF16),
        ],
        in_specs=[pl.BlockSpec(memory_space=pl.ANY)] * 6 + [pl.BlockSpec(memory_space=pltpu.SMEM)],
        out_specs=[pl.BlockSpec(memory_space=pl.ANY)] * 5,
        scratch_shapes=[
            vmem((ROWS * 16, 128), BF16),
            vmem((ROWS * 16, 128), BF16),
            vmem((ROWS * NG, 128), BF16),
            vmem((ROWS * NG, 128), BF16),
            vmem((PROWS * NG, 128), BF16),
            vmem((PROWS * NG, 128), BF16),
            vmem((ROWS * 16, 128), F32),
            vmem((2, NG, 4, 4, PIECE, 128), BF16),
            vmem((NG, NC, 2, ROWS, 128), BF16),
            vmem((NG, QROWS, 128), BF16),
            vmem((NG, QROWS, 128), BF16),
            vmem(((NPB + NRB) * BLK, QROWS), F32),
            vmem(((NPB + NRB) * BLK, QROWS), F32),
            vmem((NPB + NRB, 8, QROWS), F32),
            vmem((NG, (NPB + NRB) * BLK, QROWS), BF16),
            vmem((ROWS * 16, 128), F32),
            vmem((2, NG, NPB, BLK, 128), BF16),
            vmem((NG, NPB, BLK, 128), BF16),
            vmem((NG, 4, 4, PIECE, 128), BF16),
            vmem((NG, 4, 4, PIECE, 128), BF16),
            vmem((NG, 4, PIECE, 128), BF16),
            vmem((NG, 4, PIECE, 128), BF16),
            vmem((NG * 8, 16, 128), BF16),
            vmem((NG * 8, 16, 128), BF16),
            vmem((NG, NC, 2, ROWS, 128), BF16),
            vmem((NG, NC, 2, ROWS, 128), BF16),
            vmem((2, ROWS * NG, 128), F32),
            vmem((12 * NG, 128), F32),
            vmem((2, 12 * NG, 128), BF16),
            dma((6,)),
            dma, dma((NG,)),
            dma, dma((NG,)),
            dma, dma((NG,)),
            dma, dma((NG,)),
            dma, dma((NG, 2)),
            dma, dma((NG, 2)),
            dma, dma((NG,)),
            dma, dma((NG,)),
            dma, dma,
            dma, dma((NG, 2)),
        ],
        compiler_params=pltpu.CompilerParams(
            collective_id=0, has_side_effects=True, vmem_limit_bytes=56 * 1024 * 1024,
        ),
        name="attention_backward",
    )(
        queries.reshape(ROWS * 16, 128),
        grad_out.reshape(ROWS * 16, 128),
        resp_keys.reshape(ROWS * NG, 128),
        resp_values.reshape(ROWS * NG, 128),
        prompt_keys.reshape(PROWS * NG, 128),
        prompt_values.reshape(PROWS * NG, 128),
        resp_lengths,
    )
    anywhere = pl.BlockSpec(memory_space=pl.ANY)
    outs = pl.pallas_call(
        hand_over,
        out_shape=[jax.ShapeDtypeStruct(x.shape, x.dtype) for x in outs],
        in_specs=[anywhere] * 5,
        out_specs=[anywhere] * 5,
        scratch_shapes=[pltpu.VMEM(x.shape, x.dtype) for x in outs] + [dma((2, 5))],
        compiler_params=pltpu.CompilerParams(vmem_limit_bytes=56 * 1024 * 1024),
        name="hand_over",
    )(*outs)
    return (
        outs[0].reshape(queries.shape),
        outs[1].reshape(resp_keys.shape),
        outs[2].reshape(resp_values.shape),
        outs[3].reshape(12, NG, 128),
        outs[4].reshape(12, NG, 128),
    )


def solution(mesh):
    heads = P("resp", "ctx", "head", None)
    prompt = P("ctx", "head", None)
    owners = P(("ctx", "resp"), "head", None)
    return jax.shard_map(
        on_device,
        mesh=mesh,
        in_specs=(heads, heads, heads, heads, prompt, prompt, P("resp")),
        out_specs=(heads, heads, heads, owners, owners),
        check_vma=False,
    )
```

```python
import functools

import jax
import jax.numpy as jnp
from jax import lax
from jax.experimental import pallas as pl
from jax.experimental.pallas import tpu as pltpu
from jax.sharding import PartitionSpec as P

F32 = jnp.float32
BF16 = jnp.bfloat16
MESH = pl.DeviceIdType.MESH
SCALE = 128 ** -0.5
LOG2E = 1.4426950408889634
CEXP = SCALE * LOG2E
NG = 4
NC = 4
ROWS = 192
PROWS = 384
QROWS = 768
BLK = 384
NPB = 4
NRB = 2
PIECE = 96
LOW = -1e30
ORDER_A = (0, 1, 2, 3, 4, 5)
ORDER_C = (4, 5, 0, 1, 2, 3)


def matmul(a, b):
    return lax.dot_general(a, b, (((1,), (0,)), ((), ())), preferred_element_type=F32)


def matmul_t(a, b):
    return lax.dot_general(a, b, (((0,), (0,)), ((), ())), preferred_element_type=F32)


def kernel(
    q_hbm, do_hbm, rk_hbm, rv_hbm, pk_hbm, pv_hbm, len_ref,
    dq_out, drk_out, drv_out, dpk_out, dpv_out,
    q_raw, do_raw, rk_raw, rv_raw, pk_raw, pv_raw,
    tmp, pkv, rkv, qs, dos, e_s, w_s, m_s, ds_s, dq_s,
    s1, r1, s2, r2, s4, r4, s3, r3, sp, rp, fin_r, fin_p, fin_b,
    in_sem,
    z_send, z_recv, w_send, w_recv, x_send, x_recv, c_send, c_recv, k_send, k_recv,
    a_send, a_recv, b_send, b_recv, y_send, y_recv, o_send, o_recv, p_send, p_recv,
):
    ctx = lax.axis_index("ctx")
    resp = lax.axis_index("resp")
    core = resp % 2
    chip = resp // 2
    cx = chip // 4
    cy = chip % 4
    other = resp + 1 - 2 * core
    u = jnp.where(core == 0, cx, cy)
    v = jnp.where(core == 0, cy, cx)
    is_self = cy == 0

    def remote(src, dst, send, recv, to):
        return pltpu.make_async_remote_copy(
            src_ref=src, dst_ref=dst, send_sem=send, recv_sem=recv,
            device_id=to, device_id_type=MESH,
        )

    def ctx_at(d):
        return (ctx + d) % NC

    def plane_at(pu, pv):
        return (pu * (4 - 3 * core) + pv * (1 + 3 * core)) * 2 + core

    def u_at(d):
        return plane_at((u + d) % 4, v)

    def v_at(d):
        return plane_at(u, (v + d) % 4)

    def owner(chunk, half):
        return {"ctx": (ctx + cy) % NC, "resp": (cx * 4 + chunk) * 2 + half}

    def source(sy, kind):
        return {"ctx": (ctx + NC - sy) % NC, "resp": (cx * 4 + sy) * 2 + kind}

    barrier = pltpu.get_barrier_semaphore()

    def greet(to):
        pl.semaphore_signal(barrier, inc=1, device_id=to, device_id_type=MESH)

    loads = []
    for i, (src, dst) in enumerate(
        ((pk_hbm, pk_raw), (pv_hbm, pv_raw), (rk_hbm, rk_raw), (rv_hbm, rv_raw), (q_hbm, q_raw), (do_hbm, do_raw))
    ):
        load = pltpu.make_async_copy(src, dst, in_sem.at[i])
        load.start()
        loads.append(load)

    for d in range(1, NC):
        greet({"ctx": ctx_at(d)})

    for d in range(1, 4):
        greet({"resp": u_at(d)})
        greet({"resp": v_at(d)})
    greet({"resp": other})
    for a in range(4):
        for h in range(2):
            own_to = is_self & (core == h) if a == 0 else False

            def greet_pair(a=a, h=h):
                greet(owner(a, h))
                greet(source(a, h))

            if a == 0:
                pl.when(jnp.logical_not(own_to))(greet_pair)
            else:
                greet_pair()

    for b in range(1, NC):
        @pl.when(ctx < b)
        def _(b=b):
            for g in range(NG):
                rkv[g, b] = jnp.zeros((2, ROWS, 128), BF16)

        @pl.when((ctx >= b) | ((ctx == 0) & (b == NC - 1)))
        def _(b=b):
            for g in range(NG):
                rp[g, b] = jnp.zeros((2, ROWS, 128), BF16)

    for kind in range(2):
        loads[kind].wait()
        raw = pk_raw if kind == 0 else pv_raw
        tmp[0 : PROWS * NG, :] = raw[...].astype(F32)
        for g in range(NG):
            pkv[kind, g, 0] = tmp[pl.ds(g, PROWS, stride=NG), :].astype(BF16).reshape(4, PIECE, 128)
    for kind in range(2):
        loads[2 + kind].wait()
        raw = rk_raw if kind == 0 else rv_raw
        tmp[0 : ROWS * NG, :] = raw[...].astype(F32)
        for g in range(NG):
            rkv[g, ctx, kind] = tmp[pl.ds(g, ROWS, stride=NG), :].astype(BF16)

    @pl.when(is_self)
    def _():
        pl.semaphore_wait(barrier, 24)

    @pl.when(jnp.logical_not(is_self))
    def _():
        pl.semaphore_wait(barrier, 26)

    def z_copy(g, d):
        return remote(
            pkv.at[core, g, 0, v], pkv.at[core, g, NC - d, v],
            z_send, z_recv.at[g], {"ctx": ctx_at(d)},
        )

    def arrived(ref, sem):
        remote(ref, ref, z_send, sem, {"resp": other}).wait_recv()

    def left(ref, sem):
        remote(ref, ref, sem, z_recv.at[0], {"resp": other}).wait_send()

    def x_copy(g, d):
        part = pkv.at[core, g, pl.ds(1, 3), v]
        return remote(part, part, x_send, x_recv.at[g], {"resp": v_at(d)})

    def w_copy(d):
        part = pkv.at[core, u, pl.ds(1, 3), v]
        return remote(part, part, w_send, w_recv.at[u], {"resp": u_at(d)})

    def c_copy(g):
        part = pkv.at[core, g, pl.ds(1, 3)]
        return remote(part, part, c_send, c_recv.at[g], {"resp": other})

    def k_copy(g, to):
        return remote(
            rkv.at[g, ctx], rkv.at[g, ctx],
            k_send, k_recv.at[g, jnp.minimum(ctx, 1)], {"ctx": to},
        )

    def k_onward(g):
        return remote(rkv.at[g, 0], rkv.at[g, 0], k_send, k_recv.at[g, 0], {"ctx": 3})

    def a_copy(g, j):
        return remote(
            s1.at[1 - core, g, j], r1.at[g, j], a_send, a_recv.at[g, j // 3], {"resp": other}
        )

    def b_copy(g, to):
        return remote(
            s2.at[g, to], r2.at[g, u], b_send, b_recv.at[g], {"resp": plane_at(to, v)}
        )

    def y_copy(g, d):
        return remote(s4.at[g, (v + d) % 4], r4.at[g, v], y_send, y_recv.at[g], {"resp": v_at(d)})

    def o_copy(g, chunk, half):
        return remote(
            s3.at[g * 8 + chunk * 2 + half], r3.at[g * 8 + core * 4 + cy],
            o_send, o_recv, owner(chunk, half),
        )

    def p_copy(g, to):
        return remote(
            sp.at[g, to], rp.at[g, ctx], p_send, p_recv.at[g, 1], {"ctx": to}
        )

    def p_inward(g):
        return remote(sp.at[g, 0], rp.at[g, 0], p_send, p_recv.at[g, 0], {"ctx": 2})

    def send_resp(g):
        for c in (2, 3, 1):
            here = (ctx < c) & (ctx > 0) if c == 3 else ctx < c

            @pl.when(here)
            def _(c=c):
                k_copy(g, c).start()

    for d in range(1, NC):
        z_copy(0, d).start()

    @pl.when(u > 0)
    def _():
        for d in range(1, NC):
            z_copy(u, d).start()

    def spread_u():
        @pl.when(u > 0)
        def _():
            arrived(pkv.at[core, u, pl.ds(1, 3), v], z_recv.at[u])
            for d in range(1, NC):
                w_copy(d).start()

    def onward(g):
        @pl.when(ctx == 2)
        def _():
            arrived(rkv.at[g, 0], k_recv.at[g, 0])
            k_onward(g).start()

    def inward(g):
        @pl.when(ctx == 2)
        def _():
            arrived(rp.at[g, 0], p_recv.at[g, 0])
            total = sp[g, 0].astype(F32) + rp[g, 0].astype(F32)
            sp[g, 0] = total.astype(BF16)
            p_copy(g, 0).start()

    def forward_x(g):
        if g == 0:
            arrived(pkv.at[core, g, pl.ds(1, 3), v], z_recv.at[g])
        else:
            @pl.when(u != g)
            def _():
                arrived(pkv.at[core, g, pl.ds(1, 3), v], w_recv.at[g])

        for d in range(1, NC):
            x_copy(g, d).start()

    def forward_core(g):
        arrived(pkv.at[core, g, pl.ds(1, 3), pl.ds(0, 3)], x_recv.at[g])
        c_copy(g).start()

    length = len_ref[0]
    first = ctx * ROWS

    def take_heads(load, raw, dst, keep):
        load.wait()
        tmp[...] = raw[...].astype(F32)
        for h in range(16):
            rows = tmp[pl.ds(h, ROWS, stride=16), :]
            if keep is not None:
                rows = jnp.where(keep, rows, 0.0)
            dst[h // 4, (h % 4) * ROWS : (h % 4 + 1) * ROWS, :] = rows.astype(BF16)

    take_heads(loads[4], q_raw, qs, None)
    send_resp(0)
    forward_x(0)
    spread_u()
    position = first + lax.broadcasted_iota(jnp.int32, (ROWS, 128), 0)
    take_heads(loads[5], do_raw, dos, position < length)
    forward_core(0)
    onward(0)
    send_resp(1)
    forward_x(1)

    def key_block(g, kind, j):
        if j < NPB:
            return pkv[kind, g, j].reshape(BLK, 128)
        b = j - NPB
        return rkv[g, 2 * b : 2 * b + 2, kind].reshape(BLK, 128)

    def swap_blocks(g, blocks):
        first_block, last_block = blocks[0], blocks[-1]
        arrived(r1.at[g, pl.ds(first_block, len(blocks))], a_recv.at[g, last_block // 3])
        for j in blocks:
            total = s1[core, g, j].astype(F32) + r1[g, j].astype(F32)
            for x in range(4):
                part = total[x * PIECE : (x + 1) * PIECE].astype(BF16)
                s2[g, jnp.where(core == 0, x, j), jnp.where(core == 0, j, x)] = part
        if last_block == NPB - 1:
            for d in range(1, 4):
                b_copy(g, (u + d) % 4).start()

    def plane_send(g):
        arrived(r2.at[g, pl.ds(0, 3)], b_recv.at[g])
        total = s2[g, u].astype(F32)
        for d in range(1, 4):
            total = total + r2[g, (u + d) % 4].astype(F32)
        s4[g] = total.astype(BF16)
        for d in range(1, 4):
            y_copy(g, d).start()

    def owner_send(g):
        arrived(r4.at[g, pl.ds(0, 3)], y_recv.at[g])
        total = s4[g, v].astype(F32)
        for d in range(1, 4):
            total = total + r4[g, (v + d) % 4].astype(F32)
        total = total * jnp.where(core == 0, SCALE, 1.0)
        for chunk in range(4):
            for half in range(2):
                at = chunk * 24 + half * 8
                s3[g * 8 + chunk * 2 + half] = total[at : at + 16].astype(BF16)
        for chunk in range(4):
            for half in range(2):
                if chunk == 0:
                    mine = is_self & (core == half)

                    @pl.when(mine)
                    def _(half=half):
                        r3[g * 8 + core * 4 + cy] = s3[g * 8 + half]

                    @pl.when(jnp.logical_not(mine))
                    def _(half=half):
                        o_copy(g, 0, half).start()
                else:
                    o_copy(g, chunk, half).start()

    def below_arrived(g):
        @pl.when((ctx == 1) | (ctx == 3))
        def _():
            arrived(rkv.at[g, 0], k_recv.at[g, 0])

        @pl.when(ctx == 2)
        def _():
            arrived(rkv.at[g, 1], k_recv.at[g, 1])

        @pl.when(ctx == 3)
        def _():
            arrived(rkv.at[g, pl.ds(1, 2)], k_recv.at[g, 1])

    def send_below(g):
        @pl.when(ctx == 3)
        def _():
            p_inward(g).start()

        for c in range(NC - 1):
            here = (ctx == 1) if c == 0 else ctx > c

            @pl.when(here)
            def _(c=c):
                p_copy(g, c).start()

    def resp_finish(g):
        @pl.when(ctx < 2)
        def _():
            arrived(rp.at[g, pl.ds(0, 2)], p_recv.at[g, 1])

        @pl.when(ctx == 2)
        def _():
            arrived(rp.at[g, 3], p_recv.at[g, 1])

        for kind in range(2):
            total = sp[g, ctx, kind].astype(F32)
            for c in range(1, NC):
                total = total + rp[g, c, kind].astype(F32)
            fin_r[kind, pl.ds(g, ROWS, stride=NG), :] = total

    def middle(g):
        @pl.when(g == 0)
        def _():
            forward_x(2)

        @pl.when(g >= 1)
        def _():
            inward(g - 1)

    def later(g):
        send_below(g)

        @pl.when(g < NG - 1)
        def _():
            forward_core(g + 1)
            onward(g + 1)

        @pl.when(g < NG - 2)
        def _():
            send_resp(g + 2)

        @pl.when(g == NG - 1)
        def _():
            plane_send(g - 1)

    def ending(g):
        @pl.when(g == 0)
        def _():
            forward_x(3)

        swap_blocks(g, (3,))

        @pl.when((g >= 1) & (g < NG - 1))
        def _():
            plane_send(g - 1)

        @pl.when(g >= 2)
        def _():
            owner_send(g - 2)
            resp_finish(g - 2)

    def group(g, _):
        q = qs[g]
        do = dos[g]
        qt = q.T
        dot = do.T
        high = jnp.full((1, QROWS), LOW, F32)
        norm = jnp.zeros((1, QROWS), F32)
        delta = jnp.zeros((1, QROWS), F32)
        for j in ORDER_A:
            if j == NPB:
                below_arrived(g)
            if j == 1:
                arrived(pkv.at[1 - core, g, pl.ds(1, 3)], c_recv.at[g])
            keys = slice(j * BLK, (j + 1) * BLK)
            s = matmul(key_block(g, 0, j), qt)
            w = matmul(key_block(g, 1, j), dot)
            w_s[keys, :] = w
            if j >= NPB:
                r = lax.broadcasted_iota(jnp.int32, (BLK, QROWS), 0) + (j - NPB) * BLK
                t = lax.broadcasted_iota(jnp.int32, (1, QROWS), 1) % ROWS + first
                s = jnp.where(r <= t, s, LOW)
            new = jnp.maximum(high, jnp.max(s, axis=0, keepdims=True))
            e = jnp.exp2((s - new) * CEXP)
            e_s[keys, :] = e
            m_s[j, 0:1, :] = new
            fix = jnp.exp2((high - new) * CEXP)
            norm = norm * fix + jnp.sum(e, axis=0, keepdims=True)
            delta = delta * fix + jnp.sum(e * w, axis=0, keepdims=True)
            high = new
        inverse = 1.0 / norm
        delta = delta * inverse

        middle(g)
        for j in ORDER_C:
            keys = slice(j * BLK, (j + 1) * BLK)
            weight = jnp.exp2((m_s[j, 0:1, :] - high) * CEXP) * inverse
            p = e_s[keys, :] * weight
            ds = (p * (w_s[keys, :] - delta)).astype(BF16)
            dv = matmul(p.astype(BF16), do)
            dk = matmul(ds, q)
            if j < NPB:
                s1[0, g, j] = dk.astype(BF16)
                s1[1, g, j] = dv.astype(BF16)
                a_copy(g, j).start()
                if j == NPB - 1:
                    swap_blocks(g, (0, 1, 2))
            else:
                b = 2 * (j - NPB)
                sp[g, b : b + 2, 0] = (dk * SCALE).astype(BF16).reshape(2, ROWS, 128)
                sp[g, b : b + 2, 1] = dv.astype(BF16).reshape(2, ROWS, 128)
                if j == NPB + NRB - 1:
                    later(g)
            ds_s[g, keys, :] = ds
        ending(g)
        return 0

    lax.fori_loop(0, NG, group, 0)
    def query_part(g):
        dq = jnp.zeros((128, QROWS), F32)
        for j in range(NPB + NRB):
            dq = dq + matmul_t(key_block(g, 0, j), ds_s[g, j * BLK : (j + 1) * BLK, :])
        dq = dq.T * SCALE
        for i in range(4):
            dq_s[pl.ds(g * 4 + i, ROWS, stride=16), :] = dq[i * ROWS : (i + 1) * ROWS, :]

    query_part(0)
    owner_send(NG - 2)
    inward(NG - 1)
    query_part(1)
    query_part(2)
    plane_send(NG - 1)
    query_part(3)
    q_raw[...] = dq_s[...].astype(BF16)
    store = pltpu.make_async_copy(q_raw, dq_out, in_sem.at[0])
    store.start()
    resp_finish(NG - 2)
    owner_send(NG - 1)
    resp_finish(NG - 1)
    stores = [store]
    for kind in range(2):
        held = rk_raw if kind == 0 else rv_raw
        held[...] = fin_r[kind].astype(BF16)
        stores.append(pltpu.make_async_copy(held, drk_out if kind == 0 else drv_out, in_sem.at[1 + kind]))
        stores[-1].start()

    @pl.when(u == 0)
    def _():
        left(pkv.at[core, 0, pl.ds(0, 3), 0], z_send)

    @pl.when(u > 0)
    def _():
        left(pkv.at[core, 0, pl.ds(0, 3), pl.ds(0, 2)], z_send)
        left(pkv.at[core, 0, pl.ds(1, 3), pl.ds(0, 3)], w_send)

    left(pkv.at[core, :, pl.ds(1, 3), pl.ds(0, 3)], x_send)
    left(pkv.at[core, :, pl.ds(1, 3)], c_send)

    @pl.when(ctx < 3)
    def _():
        left(rkv.at[:, pl.ds(0, 2)], k_send)

    left(s1.at[0], a_send)
    left(s2.at[:, pl.ds(0, 3)], b_send)
    left(s4.at[:, pl.ds(0, 3)], y_send)
    for c in range(1, NC):
        @pl.when(ctx == c)
        def _(c=c):
            left(sp.at[:, pl.ds(0, c)], p_send)

    @pl.when(is_self)
    def _():
        left(s3.at[pl.ds(0, 28)], o_send)
        arrived(r3.at[pl.ds(0, 28)], o_recv)

    @pl.when(jnp.logical_not(is_self))
    def _():
        left(s3, o_send)
        arrived(r3, o_recv)

    for kind in range(2):
        for g in range(NG):
            total = r3[g * 8 + kind * 4].astype(F32)
            for su in range(1, 4):
                total = total + r3[g * 8 + kind * 4 + su].astype(F32)
            fin_p[pl.ds(g, 12, stride=NG), :] = jnp.where(core == 0, total[0:12], total[4:16])
        fin_b[kind] = fin_p[...].astype(BF16)
        stores.append(pltpu.make_async_copy(fin_b.at[kind], dpk_out if kind == 0 else dpv_out, in_sem.at[3 + kind]))
        stores[-1].start()

    for copy in stores:
        copy.wait()


def hand_over(*refs):
    sems = refs[-1]
    into = [pltpu.make_async_copy(refs[i], refs[10 + i], sems.at[0, i]) for i in range(5)]
    out = [pltpu.make_async_copy(refs[10 + i], refs[5 + i], sems.at[1, i]) for i in range(5)]
    for copy in into:
        copy.start()
    for i in range(5):
        into[i].wait()
        out[i].start()
    for copy in out:
        copy.wait()


def on_device(queries, grad_out, resp_keys, resp_values, prompt_keys, prompt_values, resp_lengths):
    dma = pltpu.SemaphoreType.DMA
    vmem = pltpu.VMEM
    outs = pl.pallas_call(
        kernel,
        out_shape=[
            jax.ShapeDtypeStruct((ROWS * 16, 128), BF16),
            jax.ShapeDtypeStruct((ROWS * NG, 128), BF16),
            jax.ShapeDtypeStruct((ROWS * NG, 128), BF16),
            jax.ShapeDtypeStruct((12 * NG, 128), BF16),
            jax.ShapeDtypeStruct((12 * NG, 128), BF16),
        ],
        in_specs=[pl.BlockSpec(memory_space=pl.ANY)] * 6 + [pl.BlockSpec(memory_space=pltpu.SMEM)],
        out_specs=[pl.BlockSpec(memory_space=pl.ANY)] * 5,
        scratch_shapes=[
            vmem((ROWS * 16, 128), BF16),
            vmem((ROWS * 16, 128), BF16),
            vmem((ROWS * NG, 128), BF16),
            vmem((ROWS * NG, 128), BF16),
            vmem((PROWS * NG, 128), BF16),
            vmem((PROWS * NG, 128), BF16),
            vmem((ROWS * 16, 128), F32),
            vmem((2, NG, 4, 4, PIECE, 128), BF16),
            vmem((NG, NC, 2, ROWS, 128), BF16),
            vmem((NG, QROWS, 128), BF16),
            vmem((NG, QROWS, 128), BF16),
            vmem(((NPB + NRB) * BLK, QROWS), F32),
            vmem(((NPB + NRB) * BLK, QROWS), F32),
            vmem((NPB + NRB, 8, QROWS), F32),
            vmem((NG, (NPB + NRB) * BLK, QROWS), BF16),
            vmem((ROWS * 16, 128), F32),
            vmem((2, NG, NPB, BLK, 128), BF16),
            vmem((NG, NPB, BLK, 128), BF16),
            vmem((NG, 4, 4, PIECE, 128), BF16),
            vmem((NG, 4, 4, PIECE, 128), BF16),
            vmem((NG, 4, PIECE, 128), BF16),
            vmem((NG, 4, PIECE, 128), BF16),
            vmem((NG * 8, 16, 128), BF16),
            vmem((NG * 8, 16, 128), BF16),
            vmem((NG, NC, 2, ROWS, 128), BF16),
            vmem((NG, NC, 2, ROWS, 128), BF16),
            vmem((2, ROWS * NG, 128), F32),
            vmem((12 * NG, 128), F32),
            vmem((2, 12 * NG, 128), BF16),
            dma((6,)),
            dma, dma((NG,)),
            dma, dma((NG,)),
            dma, dma((NG,)),
            dma, dma((NG,)),
            dma, dma((NG, 2)),
            dma, dma((NG, 2)),
            dma, dma((NG,)),
            dma, dma((NG,)),
            dma, dma,
            dma, dma((NG, 2)),
        ],
        compiler_params=pltpu.CompilerParams(
            collective_id=0, has_side_effects=True, vmem_limit_bytes=56 * 1024 * 1024,
        ),
        name="attention_backward",
    )(
        queries.reshape(ROWS * 16, 128),
        grad_out.reshape(ROWS * 16, 128),
        resp_keys.reshape(ROWS * NG, 128),
        resp_values.reshape(ROWS * NG, 128),
        prompt_keys.reshape(PROWS * NG, 128),
        prompt_values.reshape(PROWS * NG, 128),
        resp_lengths,
    )
    anywhere = pl.BlockSpec(memory_space=pl.ANY)
    outs = pl.pallas_call(
        hand_over,
        out_shape=[jax.ShapeDtypeStruct(x.shape, x.dtype) for x in outs],
        in_specs=[anywhere] * 5,
        out_specs=[anywhere] * 5,
        scratch_shapes=[pltpu.VMEM(x.shape, x.dtype) for x in outs] + [dma((2, 5))],
        compiler_params=pltpu.CompilerParams(vmem_limit_bytes=56 * 1024 * 1024),
        name="hand_over",
    )(*outs)
    return (
        outs[0].reshape(queries.shape),
        outs[1].reshape(resp_keys.shape),
        outs[2].reshape(resp_values.shape),
        outs[3].reshape(12, NG, 128),
        outs[4].reshape(12, NG, 128),
    )


def solution(mesh):
    heads = P("resp", "ctx", "head", None)
    prompt = P("ctx", "head", None)
    owners = P(("ctx", "resp"), "head", None)
    return jax.shard_map(
        on_device,
        mesh=mesh,
        in_specs=(heads, heads, heads, heads, prompt, prompt, P("resp")),
        out_specs=(heads, heads, heads, owners, owners),
        check_vma=False,
    )
```

```python
import functools

import jax
import jax.numpy as jnp
from jax import lax
from jax.experimental import pallas as pl
from jax.experimental.pallas import tpu as pltpu
from jax.sharding import PartitionSpec as P

F32 = jnp.float32
BF16 = jnp.bfloat16
MESH = pl.DeviceIdType.MESH
SCALE = 128 ** -0.5
LOG2E = 1.4426950408889634
CEXP = SCALE * LOG2E
NG = 4
NC = 4
ROWS = 192
PROWS = 384
QROWS = 768
BLK = 384
NPB = 4
NRB = 2
PIECE = 96
LOW = -1e30
ORDER_A = (0, 1, 2, 3, 4, 5)
ORDER_C = (4, 5, 0, 1, 2, 3)


def matmul(a, b):
    return lax.dot_general(a, b, (((1,), (0,)), ((), ())), preferred_element_type=F32)


def matmul_t(a, b):
    return lax.dot_general(a, b, (((0,), (0,)), ((), ())), preferred_element_type=F32)


def kernel(
    q_hbm, do_hbm, rk_hbm, rv_hbm, pk_hbm, pv_hbm, len_ref,
    dq_out, drk_out, drv_out, dpk_out, dpv_out,
    q_raw, do_raw, rk_raw, rv_raw, pk_raw, pv_raw,
    tmp, pkv, rkv, qs, dos, e_s, w_s, m_s, ds_s, dq_s,
    s1, r1, s2, r2, s4, r4, s3, r3, sp, rp, fin_r, fin_p, fin_b,
    in_sem,
    z_send, z_recv, w_send, w_recv, x_send, x_recv, c_send, c_recv, k_send, k_recv,
    a_send, a_recv, b_send, b_recv, y_send, y_recv, o_send, o_recv, p_send, p_recv,
):
    ctx = lax.axis_index("ctx")
    resp = lax.axis_index("resp")
    core = resp % 2
    chip = resp // 2
    cx = chip // 4
    cy = chip % 4
    other = resp + 1 - 2 * core
    u = jnp.where(core == 0, cx, cy)
    v = jnp.where(core == 0, cy, cx)
    is_self = cy == 0

    def remote(src, dst, send, recv, to):
        return pltpu.make_async_remote_copy(
            src_ref=src, dst_ref=dst, send_sem=send, recv_sem=recv,
            device_id=to, device_id_type=MESH,
        )

    def ctx_at(d):
        return (ctx + d) % NC

    def plane_at(pu, pv):
        return (pu * (4 - 3 * core) + pv * (1 + 3 * core)) * 2 + core

    def u_at(d):
        return plane_at((u + d) % 4, v)

    def v_at(d):
        return plane_at(u, (v + d) % 4)

    def owner(chunk, half):
        return {"ctx": (ctx + cy) % NC, "resp": (cx * 4 + chunk) * 2 + half}

    def source(sy, kind):
        return {"ctx": (ctx + NC - sy) % NC, "resp": (cx * 4 + sy) * 2 + kind}

    barrier = pltpu.get_barrier_semaphore()

    def greet(to):
        pl.semaphore_signal(barrier, inc=1, device_id=to, device_id_type=MESH)

    loads = []
    for i, (src, dst) in enumerate(
        ((pk_hbm, pk_raw), (pv_hbm, pv_raw), (rk_hbm, rk_raw), (rv_hbm, rv_raw), (q_hbm, q_raw), (do_hbm, do_raw))
    ):
        load = pltpu.make_async_copy(src, dst, in_sem.at[i])
        load.start()
        loads.append(load)

    for d in range(1, NC):
        greet({"ctx": ctx_at(d)})

    for d in range(1, 4):
        greet({"resp": u_at(d)})
        greet({"resp": v_at(d)})
    greet({"resp": other})
    for a in range(4):
        for h in range(2):
            own_to = is_self & (core == h) if a == 0 else False

            def greet_pair(a=a, h=h):
                greet(owner(a, h))
                greet(source(a, h))

            if a == 0:
                pl.when(jnp.logical_not(own_to))(greet_pair)
            else:
                greet_pair()

    for b in range(1, NC):
        @pl.when(ctx < b)
        def _(b=b):
            for g in range(NG):
                rkv[g, b] = jnp.zeros((2, ROWS, 128), BF16)

        @pl.when((ctx >= b) | ((ctx == 0) & (b == NC - 1)))
        def _(b=b):
            for g in range(NG):
                rp[g, b] = jnp.zeros((2, ROWS, 128), BF16)

    for kind in range(2):
        loads[kind].wait()
        raw = pk_raw if kind == 0 else pv_raw
        tmp[0 : PROWS * NG, :] = raw[...].astype(F32)
        for g in range(NG):
            pkv[kind, g, 0] = tmp[pl.ds(g, PROWS, stride=NG), :].astype(BF16).reshape(4, PIECE, 128)
    for kind in range(2):
        loads[2 + kind].wait()
        raw = rk_raw if kind == 0 else rv_raw
        tmp[0 : ROWS * NG, :] = raw[...].astype(F32)
        for g in range(NG):
            rkv[g, ctx, kind] = tmp[pl.ds(g, ROWS, stride=NG), :].astype(BF16)

    @pl.when(is_self)
    def _():
        pl.semaphore_wait(barrier, 24)

    @pl.when(jnp.logical_not(is_self))
    def _():
        pl.semaphore_wait(barrier, 26)

    def z_copy(g, d):
        return remote(
            pkv.at[core, g, 0, v], pkv.at[core, g, NC - d, v],
            z_send, z_recv.at[g], {"ctx": ctx_at(d)},
        )

    def arrived(ref, sem):
        remote(ref, ref, z_send, sem, {"resp": other}).wait_recv()

    def left(ref, sem):
        remote(ref, ref, sem, z_recv.at[0], {"resp": other}).wait_send()

    def x_copy(g, d):
        part = pkv.at[core, g, pl.ds(1, 3), v]
        return remote(part, part, x_send, x_recv.at[g], {"resp": v_at(d)})

    def w_copy(d):
        part = pkv.at[core, u, pl.ds(1, 3), v]
        return remote(part, part, w_send, w_recv.at[u], {"resp": u_at(d)})

    def c_copy(g):
        part = pkv.at[core, g, pl.ds(1, 3)]
        return remote(part, part, c_send, c_recv.at[g], {"resp": other})

    def k_copy(g, to):
        return remote(
            rkv.at[g, ctx], rkv.at[g, ctx],
            k_send, k_recv.at[g, jnp.minimum(ctx, 1)], {"ctx": to},
        )

    def k_onward(g):
        return remote(rkv.at[g, 0], rkv.at[g, 0], k_send, k_recv.at[g, 0], {"ctx": 3})

    def a_copy(g, j):
        return remote(
            s1.at[1 - core, g, j], r1.at[g, j], a_send, a_recv.at[g, j // 3], {"resp": other}
        )

    def b_copy(g, to):
        return remote(
            s2.at[g, to], r2.at[g, u], b_send, b_recv.at[g], {"resp": plane_at(to, v)}
        )

    def y_copy(g, d):
        return remote(s4.at[g, (v + d) % 4], r4.at[g, v], y_send, y_recv.at[g], {"resp": v_at(d)})

    def o_copy(g, chunk, half):
        return remote(
            s3.at[g * 8 + chunk * 2 + half], r3.at[g * 8 + core * 4 + cy],
            o_send, o_recv, owner(chunk, half),
        )

    def p_copy(g, to):
        return remote(
            sp.at[g, to], rp.at[g, ctx], p_send, p_recv.at[g, 1], {"ctx": to}
        )

    def p_inward(g):
        return remote(sp.at[g, 0], rp.at[g, 0], p_send, p_recv.at[g, 0], {"ctx": 2})

    def send_resp(g):
        for c in (2, 3, 1):
            here = (ctx < c) & (ctx > 0) if c == 3 else ctx < c

            @pl.when(here)
            def _(c=c):
                k_copy(g, c).start()

    for d in range(1, NC):
        z_copy(0, d).start()

    @pl.when(u > 0)
    def _():
        for d in range(1, NC):
            z_copy(u, d).start()

    def spread_u():
        @pl.when(u > 0)
        def _():
            arrived(pkv.at[core, u, pl.ds(1, 3), v], z_recv.at[u])
            for d in range(1, NC):
                w_copy(d).start()

    def onward(g):
        @pl.when(ctx == 2)
        def _():
            arrived(rkv.at[g, 0], k_recv.at[g, 0])
            k_onward(g).start()

    def inward(g):
        @pl.when(ctx == 2)
        def _():
            arrived(rp.at[g, 0], p_recv.at[g, 0])
            total = sp[g, 0].astype(F32) + rp[g, 0].astype(F32)
            sp[g, 0] = total.astype(BF16)
            p_copy(g, 0).start()

    def forward_x(g):
        if g == 0:
            arrived(pkv.at[core, g, pl.ds(1, 3), v], z_recv.at[g])
        else:
            @pl.when(u != g)
            def _():
                arrived(pkv.at[core, g, pl.ds(1, 3), v], w_recv.at[g])

        for d in range(1, NC):
            x_copy(g, d).start()

    def forward_core(g):
        arrived(pkv.at[core, g, pl.ds(1, 3), pl.ds(0, 3)], x_recv.at[g])
        c_copy(g).start()

    length = len_ref[0]
    first = ctx * ROWS

    def take_heads(load, raw, dst, keep):
        load.wait()
        tmp[...] = raw[...].astype(F32)
        for h in range(16):
            rows = tmp[pl.ds(h, ROWS, stride=16), :]
            if keep is not None:
                rows = jnp.where(keep, rows, 0.0)
            dst[h // 4, (h % 4) * ROWS : (h % 4 + 1) * ROWS, :] = rows.astype(BF16)

    take_heads(loads[4], q_raw, qs, None)
    send_resp(0)
    position = first + lax.broadcasted_iota(jnp.int32, (ROWS, 128), 0)
    take_heads(loads[5], do_raw, dos, position < length)
    forward_x(0)
    spread_u()
    forward_core(0)
    onward(0)
    send_resp(1)
    forward_x(1)

    def key_block(g, kind, j):
        if j < NPB:
            return pkv[kind, g, j].reshape(BLK, 128)
        b = j - NPB
        return rkv[g, 2 * b : 2 * b + 2, kind].reshape(BLK, 128)

    def swap_blocks(g, blocks):
        first_block, last_block = blocks[0], blocks[-1]
        arrived(r1.at[g, pl.ds(first_block, len(blocks))], a_recv.at[g, last_block // 3])
        for j in blocks:
            total = s1[core, g, j].astype(F32) + r1[g, j].astype(F32)
            for x in range(4):
                part = total[x * PIECE : (x + 1) * PIECE].astype(BF16)
                s2[g, jnp.where(core == 0, x, j), jnp.where(core == 0, j, x)] = part
        if last_block == NPB - 1:
            for d in range(1, 4):
                b_copy(g, (u + d) % 4).start()

    def plane_send(g):
        arrived(r2.at[g, pl.ds(0, 3)], b_recv.at[g])
        total = s2[g, u].astype(F32)
        for d in range(1, 4):
            total = total + r2[g, (u + d) % 4].astype(F32)
        s4[g] = total.astype(BF16)
        for d in range(1, 4):
            y_copy(g, d).start()

    def owner_send(g):
        arrived(r4.at[g, pl.ds(0, 3)], y_recv.at[g])
        total = s4[g, v].astype(F32)
        for d in range(1, 4):
            total = total + r4[g, (v + d) % 4].astype(F32)
        total = total * jnp.where(core == 0, SCALE, 1.0)
        for chunk in range(4):
            for half in range(2):
                at = chunk * 24 + half * 8
                s3[g * 8 + chunk * 2 + half] = total[at : at + 16].astype(BF16)
        for chunk in range(4):
            for half in range(2):
                if chunk == 0:
                    mine = is_self & (core == half)

                    @pl.when(mine)
                    def _(half=half):
                        r3[g * 8 + core * 4 + cy] = s3[g * 8 + half]

                    @pl.when(jnp.logical_not(mine))
                    def _(half=half):
                        o_copy(g, 0, half).start()
                else:
                    o_copy(g, chunk, half).start()

    def below_arrived(g):
        @pl.when((ctx == 1) | (ctx == 3))
        def _():
            arrived(rkv.at[g, 0], k_recv.at[g, 0])

        @pl.when(ctx == 2)
        def _():
            arrived(rkv.at[g, 1], k_recv.at[g, 1])

        @pl.when(ctx == 3)
        def _():
            arrived(rkv.at[g, pl.ds(1, 2)], k_recv.at[g, 1])

    def send_below(g):
        @pl.when(ctx == 3)
        def _():
            p_inward(g).start()

        for c in range(NC - 1):
            here = (ctx == 1) if c == 0 else ctx > c

            @pl.when(here)
            def _(c=c):
                p_copy(g, c).start()

    def resp_finish(g):
        @pl.when(ctx < 2)
        def _():
            arrived(rp.at[g, pl.ds(0, 2)], p_recv.at[g, 1])

        @pl.when(ctx == 2)
        def _():
            arrived(rp.at[g, 3], p_recv.at[g, 1])

        for kind in range(2):
            total = sp[g, ctx, kind].astype(F32)
            for c in range(1, NC):
                total = total + rp[g, c, kind].astype(F32)
            fin_r[kind, pl.ds(g, ROWS, stride=NG), :] = total

    def middle(g):
        @pl.when(g == 0)
        def _():
            forward_x(2)

        @pl.when(g >= 1)
        def _():
            inward(g - 1)

    def later(g):
        send_below(g)

        @pl.when(g < NG - 1)
        def _():
            forward_core(g + 1)
            onward(g + 1)

        @pl.when(g < NG - 2)
        def _():
            send_resp(g + 2)

        @pl.when(g == NG - 1)
        def _():
            plane_send(g - 1)

    def ending(g):
        @pl.when(g == 0)
        def _():
            forward_x(3)

        @pl.when(g == NG - 1)
        def _():
            swap_blocks(g, (3,))

        @pl.when((g >= 1) & (g < NG - 1))
        def _():
            plane_send(g - 1)

        @pl.when(g >= 2)
        def _():
            owner_send(g - 2)
            resp_finish(g - 2)

    def group(g, _):
        q = qs[g]
        do = dos[g]
        qt = q.T
        dot = do.T
        high = jnp.full((1, QROWS), LOW, F32)
        norm = jnp.zeros((1, QROWS), F32)
        delta = jnp.zeros((1, QROWS), F32)
        for j in ORDER_A:
            if j == NPB:
                below_arrived(g)
            if j == 1:
                @pl.when(g >= 1)
                def _():
                    swap_blocks(g - 1, (0, 1, 2))
                    swap_blocks(g - 1, (3,))

                arrived(pkv.at[1 - core, g, pl.ds(1, 3)], c_recv.at[g])
            keys = slice(j * BLK, (j + 1) * BLK)
            s = matmul(key_block(g, 0, j), qt)
            w = matmul(key_block(g, 1, j), dot)
            w_s[keys, :] = w
            if j >= NPB:
                r = lax.broadcasted_iota(jnp.int32, (BLK, QROWS), 0) + (j - NPB) * BLK
                t = lax.broadcasted_iota(jnp.int32, (1, QROWS), 1) % ROWS + first
                s = jnp.where(r <= t, s, LOW)
            new = jnp.maximum(high, jnp.max(s, axis=0, keepdims=True))
            e = jnp.exp2((s - new) * CEXP)
            e_s[keys, :] = e
            m_s[j, 0:1, :] = new
            fix = jnp.exp2((high - new) * CEXP)
            norm = norm * fix + jnp.sum(e, axis=0, keepdims=True)
            delta = delta * fix + jnp.sum(e * w, axis=0, keepdims=True)
            high = new
        inverse = 1.0 / norm
        delta = delta * inverse

        middle(g)
        for j in ORDER_C:
            keys = slice(j * BLK, (j + 1) * BLK)
            weight = jnp.exp2((m_s[j, 0:1, :] - high) * CEXP) * inverse
            p = e_s[keys, :] * weight
            ds = (p * (w_s[keys, :] - delta)).astype(BF16)
            dv = matmul(p.astype(BF16), do)
            dk = matmul(ds, q)
            if j < NPB:
                s1[0, g, j] = dk.astype(BF16)
                s1[1, g, j] = dv.astype(BF16)
                a_copy(g, j).start()
                if j == NPB - 1:
                    @pl.when(g == NG - 1)
                    def _():
                        swap_blocks(g, (0, 1, 2))
            else:
                b = 2 * (j - NPB)
                sp[g, b : b + 2, 0] = (dk * SCALE).astype(BF16).reshape(2, ROWS, 128)
                sp[g, b : b + 2, 1] = dv.astype(BF16).reshape(2, ROWS, 128)
                if j == NPB + NRB - 1:
                    later(g)
            ds_s[g, keys, :] = ds
        ending(g)
        return 0

    lax.fori_loop(0, NG, group, 0)
    def query_part(g):
        dq = jnp.zeros((128, QROWS), F32)
        for j in range(NPB + NRB):
            dq = dq + matmul_t(key_block(g, 0, j), ds_s[g, j * BLK : (j + 1) * BLK, :])
        dq = dq.T * SCALE
        for i in range(4):
            dq_s[pl.ds(g * 4 + i, ROWS, stride=16), :] = dq[i * ROWS : (i + 1) * ROWS, :]

    query_part(0)
    owner_send(NG - 2)
    inward(NG - 1)
    query_part(1)
    query_part(2)
    plane_send(NG - 1)
    query_part(3)
    q_raw[...] = dq_s[...].astype(BF16)
    store = pltpu.make_async_copy(q_raw, dq_out, in_sem.at[0])
    store.start()
    resp_finish(NG - 2)
    owner_send(NG - 1)
    resp_finish(NG - 1)
    stores = [store]
    for kind in range(2):
        held = rk_raw if kind == 0 else rv_raw
        held[...] = fin_r[kind].astype(BF16)
        stores.append(pltpu.make_async_copy(held, drk_out if kind == 0 else drv_out, in_sem.at[1 + kind]))
        stores[-1].start()

    @pl.when(u == 0)
    def _():
        left(pkv.at[core, 0, pl.ds(0, 3), 0], z_send)

    @pl.when(u > 0)
    def _():
        left(pkv.at[core, 0, pl.ds(0, 3), pl.ds(0, 2)], z_send)
        left(pkv.at[core, 0, pl.ds(1, 3), pl.ds(0, 3)], w_send)

    left(pkv.at[core, :, pl.ds(1, 3), pl.ds(0, 3)], x_send)
    left(pkv.at[core, :, pl.ds(1, 3)], c_send)

    @pl.when(ctx < 3)
    def _():
        left(rkv.at[:, pl.ds(0, 2)], k_send)

    left(s1.at[0], a_send)
    left(s2.at[:, pl.ds(0, 3)], b_send)
    left(s4.at[:, pl.ds(0, 3)], y_send)
    for c in range(1, NC):
        @pl.when(ctx == c)
        def _(c=c):
            left(sp.at[:, pl.ds(0, c)], p_send)

    @pl.when(is_self)
    def _():
        left(s3.at[pl.ds(0, 28)], o_send)
        arrived(r3.at[pl.ds(0, 28)], o_recv)

    @pl.when(jnp.logical_not(is_self))
    def _():
        left(s3, o_send)
        arrived(r3, o_recv)

    for kind in range(2):
        for g in range(NG):
            total = r3[g * 8 + kind * 4].astype(F32)
            for su in range(1, 4):
                total = total + r3[g * 8 + kind * 4 + su].astype(F32)
            fin_p[pl.ds(g, 12, stride=NG), :] = jnp.where(core == 0, total[0:12], total[4:16])
        fin_b[kind] = fin_p[...].astype(BF16)
        stores.append(pltpu.make_async_copy(fin_b.at[kind], dpk_out if kind == 0 else dpv_out, in_sem.at[3 + kind]))
        stores[-1].start()

    for copy in stores:
        copy.wait()


def hand_over(*refs):
    sems = refs[-1]
    into = [pltpu.make_async_copy(refs[i], refs[10 + i], sems.at[0, i]) for i in range(5)]
    out = [pltpu.make_async_copy(refs[10 + i], refs[5 + i], sems.at[1, i]) for i in range(5)]
    for copy in into:
        copy.start()
    for i in range(5):
        into[i].wait()
        out[i].start()
    for copy in out:
        copy.wait()


def on_device(queries, grad_out, resp_keys, resp_values, prompt_keys, prompt_values, resp_lengths):
    dma = pltpu.SemaphoreType.DMA
    vmem = pltpu.VMEM
    outs = pl.pallas_call(
        kernel,
        out_shape=[
            jax.ShapeDtypeStruct((ROWS * 16, 128), BF16),
            jax.ShapeDtypeStruct((ROWS * NG, 128), BF16),
            jax.ShapeDtypeStruct((ROWS * NG, 128), BF16),
            jax.ShapeDtypeStruct((12 * NG, 128), BF16),
            jax.ShapeDtypeStruct((12 * NG, 128), BF16),
        ],
        in_specs=[pl.BlockSpec(memory_space=pl.ANY)] * 6 + [pl.BlockSpec(memory_space=pltpu.SMEM)],
        out_specs=[pl.BlockSpec(memory_space=pl.ANY)] * 5,
        scratch_shapes=[
            vmem((ROWS * 16, 128), BF16),
            vmem((ROWS * 16, 128), BF16),
            vmem((ROWS * NG, 128), BF16),
            vmem((ROWS * NG, 128), BF16),
            vmem((PROWS * NG, 128), BF16),
            vmem((PROWS * NG, 128), BF16),
            vmem((ROWS * 16, 128), F32),
            vmem((2, NG, 4, 4, PIECE, 128), BF16),
            vmem((NG, NC, 2, ROWS, 128), BF16),
            vmem((NG, QROWS, 128), BF16),
            vmem((NG, QROWS, 128), BF16),
            vmem(((NPB + NRB) * BLK, QROWS), F32),
            vmem(((NPB + NRB) * BLK, QROWS), F32),
            vmem((NPB + NRB, 8, QROWS), F32),
            vmem((NG, (NPB + NRB) * BLK, QROWS), BF16),
            vmem((ROWS * 16, 128), F32),
            vmem((2, NG, NPB, BLK, 128), BF16),
            vmem((NG, NPB, BLK, 128), BF16),
            vmem((NG, 4, 4, PIECE, 128), BF16),
            vmem((NG, 4, 4, PIECE, 128), BF16),
            vmem((NG, 4, PIECE, 128), BF16),
            vmem((NG, 4, PIECE, 128), BF16),
            vmem((NG * 8, 16, 128), BF16),
            vmem((NG * 8, 16, 128), BF16),
            vmem((NG, NC, 2, ROWS, 128), BF16),
            vmem((NG, NC, 2, ROWS, 128), BF16),
            vmem((2, ROWS * NG, 128), F32),
            vmem((12 * NG, 128), F32),
            vmem((2, 12 * NG, 128), BF16),
            dma((6,)),
            dma, dma((NG,)),
            dma, dma((NG,)),
            dma, dma((NG,)),
            dma, dma((NG,)),
            dma, dma((NG, 2)),
            dma, dma((NG, 2)),
            dma, dma((NG,)),
            dma, dma((NG,)),
            dma, dma,
            dma, dma((NG, 2)),
        ],
        compiler_params=pltpu.CompilerParams(
            collective_id=0, has_side_effects=True, vmem_limit_bytes=56 * 1024 * 1024,
        ),
        name="attention_backward",
    )(
        queries.reshape(ROWS * 16, 128),
        grad_out.reshape(ROWS * 16, 128),
        resp_keys.reshape(ROWS * NG, 128),
        resp_values.reshape(ROWS * NG, 128),
        prompt_keys.reshape(PROWS * NG, 128),
        prompt_values.reshape(PROWS * NG, 128),
        resp_lengths,
    )
    anywhere = pl.BlockSpec(memory_space=pl.ANY)
    outs = pl.pallas_call(
        hand_over,
        out_shape=[jax.ShapeDtypeStruct(x.shape, x.dtype) for x in outs],
        in_specs=[anywhere] * 5,
        out_specs=[anywhere] * 5,
        scratch_shapes=[pltpu.VMEM(x.shape, x.dtype) for x in outs] + [dma((2, 5))],
        compiler_params=pltpu.CompilerParams(vmem_limit_bytes=56 * 1024 * 1024),
        name="hand_over",
    )(*outs)
    return (
        outs[0].reshape(queries.shape),
        outs[1].reshape(resp_keys.shape),
        outs[2].reshape(resp_values.shape),
        outs[3].reshape(12, NG, 128),
        outs[4].reshape(12, NG, 128),
    )


def solution(mesh):
    heads = P("resp", "ctx", "head", None)
    prompt = P("ctx", "head", None)
    owners = P(("ctx", "resp"), "head", None)
    return jax.shard_map(
        on_device,
        mesh=mesh,
        in_specs=(heads, heads, heads, heads, prompt, prompt, P("resp")),
        out_specs=(heads, heads, heads, owners, owners),
        check_vma=False,
    )
```
